256 devices in a mesh: stn: 16 (over z, x_hi), tf: 16 (over y, x_lo, core).
Axes of the slice: x: 4 (x_hi: 2, x_lo: 2; x = x_hi * 2 + x_lo), y: 4, z: 8, core: 2. Of those that a mesh axis runs over, the one named last changes fastest.
Arguments:
- voltages: bfloat16 [2, 128, 2, 524288], P(None, 'stn', None, 'tf'), may hold values from -6 to 6
- delay_table: float32 [128, 128], replicated, may hold values from -512 to 512
- beam_pointing: int32 [32], replicated, may hold values from 0 to 127
- station_group: int32 [128], replicated, may hold values from 0 to 3
Outputs:
- beams: bfloat16 [32, 2, 2, 128, 32, 128], P('stn', None, None, None, 'tf')
The draws below stay inside these ranges and needn't reach their ends.
All inputs are finite; a program needn't handle non-finite values.
Results may differ from the reference program's by a relative error of at most 0.0082.
Values may be sent and summed in bfloat16 or wider, within the bound.
A program may use at most 128 MiB of HBM per device.

```python
import math
import jax
import jax.numpy as jnp
from jax import lax

TAPS = 16
CH_LO = 32
CH_HI = 128
BEAMS = 32
GROUPS = 4
DIRS = 128
STATIONS = 128
FRAMES = 128
SAMPLES = 524288


def place_ends(array, stream_key, smallest, largest):
    place = [jax.random.randint(jax.random.fold_in(stream_key, axis), (), 0, length) for axis, length in enumerate(array.shape)]
    longest = array.shape.index(max(array.shape))
    neighbour = place[:longest] + [(place[longest] + 1) % array.shape[longest]] + place[longest + 1:]
    return array.at[tuple(place)].set(smallest).at[tuple(neighbour)].set(largest)


def levels(stream_key, extent, shards, low, top_value):
    level, own = 1.0, jax.random.fold_in(stream_key, 6)
    for axis_at, blocks in shards:
        heights = jnp.exp(jax.random.uniform(jax.random.fold_in(own, axis_at), (blocks,), jnp.float32, low / len(shards), top_value / len(shards)))
        level = level * jnp.repeat(heights, extent[axis_at] // blocks).reshape([-1 if axis == axis_at else 1 for axis in range(len(extent))])
    return level


def centred(rng, dims, width, reach, pieces=(), kind=jnp.bfloat16):
    drawn = width * jax.random.normal(rng, dims, jnp.float32)
    if pieces:
        drawn = drawn * levels(rng, dims, pieces, -0.22, 0.18)
    return jnp.clip(drawn, -reach, reach).astype(kind)


def setup_inputs(seed: int = 0) -> dict:
    key_of = jax.random.split(jax.random.key(seed), 5)
    return {
        "voltages": centred(key_of[0], (2, STATIONS, 2, SAMPLES), 1.0, 6.0, ((1, 16), (3, 16))),
        "delay_table": jnp.clip(jax.random.uniform(key_of[1], (DIRS, STATIONS), jnp.float32, -512.0, 512.0), -512.0, 512.0),
        "beam_pointing": place_ends(jax.random.randint(key_of[2], (BEAMS,), 0, DIRS), jax.random.fold_in(key_of[2], 1), 0, DIRS - 1).astype(jnp.int32),
        "station_group": place_ends(jax.random.randint(key_of[3], (STATIONS,), 0, GROUPS), jax.random.fold_in(key_of[3], 1), 0, GROUPS - 1).astype(jnp.int32),
    }


TWO_PI = 2.0 * math.pi

def filter_window(tap_count, points):
    position = jnp.arange(tap_count * points, dtype=jnp.int32).astype(jnp.float32)
    total_len = float(tap_count * points)
    hann_taper = 0.5 - 0.5 * jnp.cos(TWO_PI / total_len * position)
    kernel = jnp.sinc((position - 0.5 * total_len) / float(points)) * hann_taper
    return kernel.reshape(tap_count, points)

def dft_table(points):
    counter = jnp.arange(points, dtype=jnp.int32)
    product = counter[:, None] * counter[None, :] % points
    angles = TWO_PI / points * product.astype(jnp.float32)
    factor = 1.0 / math.sqrt(points)
    cosine = jnp.cos(angles) * factor
    sine_part = jnp.sin(angles) * factor
    stacked = jnp.stack([jnp.stack([cosine, sine_part]), jnp.stack([-sine_part, cosine])])
    return stacked.astype(jnp.bfloat16)

def channelize(extended, frame_count):
    points = CH_LO * CH_HI
    window = filter_window(TAPS, points)
    filtered = sum((window[tap_step] * extended[:, :, :, tap_step:tap_step + frame_count, :].astype(jnp.float32) for tap_step in range(TAPS)))
    filtered = filtered.astype(jnp.bfloat16)
    shaped = filtered.reshape(filtered.shape[:4] + (CH_LO, CH_HI))
    section_one = jnp.einsum('oikn,ispfnm->ospfkm', dft_table(CH_LO).astype(jnp.float32), shaped.astype(jnp.float32))
    low_index = jnp.arange(CH_LO, dtype=jnp.int32)
    high_index = jnp.arange(CH_HI, dtype=jnp.int32)
    twiddle = TWO_PI / points * (low_index[:, None] * high_index[None, :]).astype(jnp.float32)
    cosine = jnp.cos(twiddle)
    sine_part = jnp.sin(twiddle)
    rotated = jnp.stack([section_one[0] * cosine + section_one[1] * sine_part, section_one[1] * cosine - section_one[0] * sine_part]).astype(jnp.bfloat16)
    return jnp.einsum('oimj,ispfkm->ospfkj', dft_table(CH_HI).astype(jnp.float32), rotated.astype(jnp.float32)).astype(jnp.bfloat16)

def beam_weights(delays, beam_ids, groups, channel_low, station_total):
    points = CH_LO * CH_HI
    member = (groups[None, :] == (beam_ids % GROUPS)[:, None]).astype(jnp.float32)
    weight_scale = math.sqrt(GROUPS / station_total) * member
    channel = channel_low[:, None] + CH_LO * jnp.arange(CH_HI, dtype=jnp.int32)[None, :]
    fraction = channel.astype(jnp.float32) / float(points)
    phases = TWO_PI * (delays[:, :, None, None] * fraction[None, None])
    weight_re = (weight_scale[:, :, None, None] * jnp.cos(phases)).astype(jnp.bfloat16)
    weight_im = (-weight_scale[:, :, None, None] * jnp.sin(phases)).astype(jnp.bfloat16)
    return (weight_re, weight_im)

def form_beams(weight_re, weight_im, channels):
    real_in = channels[0]
    imag_in = channels[1]

    def contract(weights_part, data_part):
        return jnp.einsum('bsxc,spfxc->bpfxc', weights_part.astype(jnp.float32), data_part.astype(jnp.float32))
    real_out = contract(weight_re, real_in) - contract(weight_im, imag_in)
    imag_out = contract(weight_re, imag_in) + contract(weight_im, real_in)
    return jnp.stack([real_out, imag_out], axis=1)

def reference(voltages, delay_table, beam_pointing, station_group):
    points = CH_LO * CH_HI

    def one_station(samples):
        framed = samples.reshape(2, 1, 2, FRAMES, points)
        padded = jnp.concatenate([jnp.zeros((2, 1, 2, TAPS - 1, points), samples.dtype), framed], axis=3)
        return channelize(padded, FRAMES)[:, 0]
    per_station = lax.map(one_station, jnp.moveaxis(voltages, 1, 0))
    delays = delay_table[beam_pointing]
    beam_ids = jnp.arange(BEAMS, dtype=jnp.int32)

    def one_low(low_pick):
        sliced = lax.dynamic_index_in_dim(per_station, low_pick, 4, keepdims=True)
        sliced = jnp.moveaxis(sliced, 1, 0)
        channel_low = jnp.reshape(low_pick, (1,)).astype(jnp.int32)
        weight_re, weight_im = beam_weights(delays, beam_ids, station_group, channel_low, STATIONS)
        return form_beams(weight_re, weight_im, sliced)[:, :, :, :, 0, :].astype(jnp.bfloat16)
    stacked = lax.map(one_low, jnp.arange(CH_LO, dtype=jnp.int32))
    return jnp.moveaxis(stacked, 0, 4)
```

```python
import math

import jax
import jax.numpy as jnp
import numpy as np
from jax import lax
from jax.experimental import pallas as pl
from jax.experimental.pallas import tpu as pltpu
from jax.sharding import PartitionSpec as P

TAPS = 16
CH_LO = 32
CH_HI = 128
POINTS = CH_LO * CH_HI
GROUPS = 4
TWO_PI = 2.0 * math.pi
BF = jnp.bfloat16
F32 = jnp.float32
MESH = pl.DeviceIdType.MESH

N = 16
FRAMES_OWN = 8
STEPS = 8
BB = 8


def filter_window():
    position = jnp.arange(TAPS * POINTS, dtype=jnp.int32).astype(F32)
    total = float(TAPS * POINTS)
    taper = 0.5 - 0.5 * jnp.cos(TWO_PI / total * position)
    kernel = jnp.sinc((position - 0.5 * total) / float(POINTS)) * taper
    return kernel.reshape(TAPS, CH_LO, CH_HI)


def dft_table(points):
    counter = np.arange(points)
    angles = 2.0 * np.pi / points * (counter[:, None] * counter[None, :] % points)
    cosine = np.cos(angles) / math.sqrt(points)
    sine = np.sin(angles) / math.sqrt(points)
    return np.stack([np.stack([cosine, sine]), np.stack([-sine, cosine])])


def low_matrix():
    table = dft_table(CH_LO)
    eye = np.eye(8)
    full = np.einsum("oqkn,fg->kofgqn", table, eye)
    return jnp.asarray(full.reshape(512, 512).astype(np.float32)).astype(BF)


def high_matrix():
    table = dft_table(CH_HI)
    return jnp.asarray(
        table.transpose(1, 2, 0, 3).reshape(256, 256).astype(np.float32)
    ).astype(BF)


def twiddle_table():
    angle = 2.0 * np.pi / POINTS * (np.arange(CH_LO)[:, None] * np.arange(CH_HI)[None, :])
    pair = np.stack([np.cos(angle), np.sin(angle)], axis=1)
    return jnp.asarray(np.concatenate([pair, pair], axis=-1).astype(np.float32))


def turn_parts(turns):
    t = (turns - jnp.round(turns)) * math.pi
    y = t * t
    s = t * (
        1.0
        + y
        * (
            -1.0 / 6
            + y
            * (
                1.0 / 120
                + y * (-1.0 / 5040 + y * (1.0 / 362880 + y * (-1.0 / 39916800 + y / 6227020800.0)))
            )
        )
    )
    c = 1.0 + y * (
        -0.5
        + y
        * (
            1.0 / 24
            + y
            * (
                -1.0 / 720
                + y * (1.0 / 40320 + y * (-1.0 / 3628800 + y * (1.0 / 479001600)))
            )
        )
    )
    return 1.0 - 2.0 * s * s, 2.0 * s * c


def z_shift(step):
    k = 7 - step
    half = (k + 1) // 2
    return half * (2 * (k % 2) - 1)


def fused(
    xv, win, low, high, twid, delay, member,
    out,
    rbuf, filt, chan, recv, weights, acc, csend,
    send_a, recv_a, send_b, recv_b, send_c, recv_c,
):
    i = lax.axis_index("stn")
    j = lax.axis_index("tf")
    z = i // 2
    parity = j % 2

    own_a = pltpu.make_async_copy(xv.at[j], rbuf.at[pl.ds(16 + 8 * j, 8)], recv_a)
    own_a.start()

    def send_voltages(step, carry):
        target = lax.rem(j + step, N)
        pltpu.make_async_remote_copy(
            src_ref=xv.at[target],
            dst_ref=rbuf.at[pl.ds(16 + 8 * j, 8)],
            send_sem=send_a,
            recv_sem=recv_a,
            device_id=(i, target),
            device_id_type=MESH,
        ).start()
        return carry

    lax.fori_loop(1, N, send_voltages, 0)

    rbuf[pl.ds(0, 16)] = jnp.zeros((16, 2, CH_LO, CH_HI), BF)
    acc[...] = jnp.zeros(acc.shape, F32)

    lane = lax.broadcasted_iota(jnp.int32, (8, CH_HI), 1)
    lane4 = lax.broadcasted_iota(jnp.int32, (GROUPS, CH_HI), 1)

    def make_weights(s, carry):
        column = jnp.sum(jnp.where(lane == s, delay[...], 0.0), axis=1, keepdims=True)
        scale = jnp.sum(jnp.where(lane4 == s, member[...], 0.0), axis=1, keepdims=True)
        for k2 in range(2):
            channel = (2 * j + k2) + CH_LO * lane
            fraction = channel.astype(F32) * (1.0 / POINTS)
            cosine, sine = turn_parts(column * fraction)
            for g in range(GROUPS):
                amount = scale[g : g + 1, :]
                weights[s, k2, 0, pl.ds(8 * g, 8), :] = (amount * cosine).astype(BF).astype(F32)
                weights[s, k2, 1, pl.ds(8 * g, 8), :] = (amount * -sine).astype(BF).astype(F32)
        return carry

    lax.fori_loop(0, 128, make_weights, 0)

    pltpu.make_async_copy(rbuf.at[pl.ds(16, 128)], rbuf.at[pl.ds(16, 128)], recv_a).wait()

    def block(step, carry):
        fb = lax.rem(z + z_shift(step) + 8, 8)
        i_to = 2 * fb + parity

        def filter_part(part, inner):
            q = part // 2
            row = pl.multiple_of((part % 2) * 16, 16)
            for g2 in range(2):
                base = fb * 16 + g2 * 8
                sums = [None] * 8
                taps = [win[t, pl.ds(row, 16), :] for t in range(TAPS)]
                for k in range(1, 24):
                    x = rbuf[base + k, q, pl.ds(row, 16), :].astype(F32)
                    for f in range(8):
                        t = k - 1 - f
                        if 0 <= t < TAPS:
                            term = taps[t] * x
                            sums[f] = term if sums[f] is None else sums[f] + term
                for f in range(8):
                    filt[pl.ds(pl.multiple_of(f * 64 + q * 32 + row, 16), 16), pl.ds(128 * g2, 128)] = sums[f].astype(BF)
            return inner

        lax.fori_loop(0, 4, filter_part, 0)

        def transform(part, inner):
            c = lax.rem(part + j // 4, 4)
            first = jnp.dot(
                low[pl.ds(pl.multiple_of(c * 128, 128), 128), :], filt[...], preferred_element_type=F32
            ).reshape(8, 2, 8, 256)
            table = twid[pl.ds(c * 8, 8)]
            cosine, sine = table[:, 0:1, :], table[:, 1:2, :]
            re = first[:, 0] * cosine + first[:, 1] * sine
            im = first[:, 1] * cosine - first[:, 0] * sine
            re = jnp.concatenate([re[:, :, :128], re[:, :, 128:]], axis=1).astype(BF)
            im = jnp.concatenate([im[:, :, :128], im[:, :, 128:]], axis=1).astype(BF)
            rotated = jnp.concatenate([re, im], axis=2).reshape(128, 256)
            done = jnp.dot(rotated, high[...], preferred_element_type=F32).astype(BF)
            chan[step, pl.ds(c * 8, 8)] = done.reshape(8, 16, 256)

            def send(n, deep):
                j_to = c * 4 + lax.rem(n + j, 4)
                here = jnp.logical_and(i_to == i, j_to == j)
                source = chan.at[step, pl.ds(2 * j_to, 2)]
                target = recv.at[8 * i + j // 2]

                @pl.when(here)
                def _():
                    pltpu.make_async_copy(source, target, recv_b.at[i]).start()

                @pl.when(jnp.logical_not(here))
                def _():
                    pltpu.make_async_remote_copy(
                        src_ref=source,
                        dst_ref=target,
                        send_sem=send_b.at[step],
                        recv_sem=recv_b.at[i],
                        device_id=(i_to, j_to),
                        device_id_type=MESH,
                    ).start()

                return deep

            lax.fori_loop(0, 4, send, 0)
            return inner

        lax.fori_loop(0, 4, transform, 0)
        return carry

    lax.fori_loop(0, STEPS, block, 0)

    def add_block(step, carry):
        z_from = lax.rem(z - z_shift(step // 2) + 8, 8)
        i_from = 2 * z_from + step % 2
        s0 = 8 * i_from
        pltpu.make_async_copy(recv.at[pl.ds(s0, 8)], recv.at[pl.ds(s0, 8)], recv_b.at[i_from]).wait()

        def part(n, inner):
            k2 = n // 4
            g = n % 4
            re = [acc[k2, g, b, 0] for b in range(BB)]
            im = [acc[k2, g, b, 1] for b in range(BB)]
            for s in range(8):
                value = recv[s0 + s, k2].astype(F32)
                vr, vi = value[:, :128], value[:, 128:]
                for b in range(BB):
                    wr = weights[s0 + s, k2, 0, pl.ds(8 * g + b, 1), :]
                    wi = weights[s0 + s, k2, 1, pl.ds(8 * g + b, 1), :]
                    re[b] = re[b] + (wr * vr - wi * vi)
                    im[b] = im[b] + (wr * vi + wi * vr)
            for b in range(BB):
                acc[k2, g, b, 0] = re[b]
                acc[k2, g, b, 1] = im[b]
            return inner

        lax.fori_loop(0, 8, part, 0)
        return carry

    lax.fori_loop(0, N, add_block, 0)

    for k2 in range(2):
        for g in range(GROUPS):
            for b in range(BB):
                for q in range(2):
                    csend[2 * b + g // 2, g % 2, q, k2] = acc[k2, g, b, q].astype(BF)

    own_c = pltpu.make_async_copy(csend.at[i], out.at[i], recv_c)
    own_c.start()

    def send_beams(step, carry):
        target = lax.rem(i + step, N)
        pltpu.make_async_remote_copy(
            src_ref=csend.at[target],
            dst_ref=out.at[i],
            send_sem=send_c,
            recv_sem=recv_c,
            device_id=(target, j),
            device_id_type=MESH,
        ).start()
        return carry

    lax.fori_loop(1, N, send_beams, 0)

    pltpu.make_async_copy(rbuf.at[pl.ds(0, 120)], rbuf.at[pl.ds(0, 120)], send_a).wait()

    def wait_sent(step, carry):
        fb = lax.rem(z + z_shift(step) + 8, 8)
        mine = jnp.logical_and(2 * fb + parity == i, True)

        @pl.when(mine)
        def _():
            pltpu.make_async_copy(
                chan.at[step, pl.ds(0, 30)], chan.at[step, pl.ds(0, 30)], send_b.at[step]
            ).wait()

        @pl.when(jnp.logical_not(mine))
        def _():
            pltpu.make_async_copy(chan.at[step], chan.at[step], send_b.at[step]).wait()

        return carry

    lax.fori_loop(0, STEPS, wait_sent, 0)
    pltpu.make_async_copy(csend.at[pl.ds(0, 15)], csend.at[pl.ds(0, 15)], send_c).wait()
    pltpu.make_async_copy(csend, csend, recv_c).wait()


def body(voltages, delay_table, beam_pointing, station_group):
    stations_here = voltages.shape[1]
    parts = voltages.reshape(2, stations_here, 2, FRAMES_OWN, CH_LO, CH_HI)
    xv = parts.transpose(1, 2, 3, 0, 4, 5).reshape(N, FRAMES_OWN, 2, CH_LO, CH_HI)

    stations = station_group.shape[0]
    delays = jnp.take(delay_table, beam_pointing, axis=0, mode="clip")
    delays = delays.reshape(BB, GROUPS, stations)
    groups = jnp.arange(GROUPS, dtype=jnp.int32)
    own = station_group[None, :] == groups[:, None]
    delay = jnp.sum(jnp.where(own[None], delays, 0.0), axis=1)
    member = math.sqrt(GROUPS / stations) * own.astype(F32)

    vmem = pl.BlockSpec(memory_space=pltpu.VMEM)
    anywhere = pl.BlockSpec(memory_space=pl.ANY)
    out = pl.pallas_call(
        fused,
        out_shape=jax.ShapeDtypeStruct((N, 2, 2, 2, 16, CH_HI), BF),
        in_specs=[anywhere] + [vmem] * 6,
        out_specs=anywhere,
        scratch_shapes=[
            pltpu.VMEM((144, 2, CH_LO, CH_HI), BF),
            pltpu.VMEM((512, 256), BF),
            pltpu.VMEM((STEPS, CH_LO, 16, 256), BF),
            pltpu.VMEM((128, 2, 16, 256), BF),
            pltpu.VMEM((128, 2, 2, 32, CH_HI), F32),
            pltpu.VMEM((2, GROUPS, BB, 2, 16, CH_HI), F32),
            pltpu.VMEM((N, 2, 2, 2, 16, CH_HI), BF),
            pltpu.SemaphoreType.DMA,
            pltpu.SemaphoreType.DMA,
            pltpu.SemaphoreType.DMA((STEPS,)),
            pltpu.SemaphoreType.DMA((N,)),
            pltpu.SemaphoreType.DMA,
            pltpu.SemaphoreType.DMA,
        ],
        compiler_params=pltpu.CompilerParams(
            has_side_effects=True, vmem_limit_bytes=40 * 1024 * 1024
        ),
        name="channelize_and_beamform",
    )(xv, filter_window(), low_matrix(), high_matrix(), twiddle_table(), delay, member)

    out = out.reshape(8, 2, 2, 2, 2, 16, CH_HI).transpose(2, 3, 1, 0, 5, 4, 6)
    return out.reshape(2, 2, 2, 128, 2, CH_HI)


def solution(mesh):
    in_specs = (P(None, "stn", None, "tf"), P(), P(), P())
    out_specs = P("stn", None, None, None, "tf", None)
    return jax.shard_map(body, mesh=mesh, in_specs=in_specs, out_specs=out_specs, check_vma=False)
```

```python
import math

import jax
import jax.numpy as jnp
import numpy as np
from jax import lax
from jax.experimental import pallas as pl
from jax.experimental.pallas import tpu as pltpu
from jax.sharding import PartitionSpec as P

TAPS = 16
CH_LO = 32
CH_HI = 128
POINTS = CH_LO * CH_HI
GROUPS = 4
TWO_PI = 2.0 * math.pi
BF = jnp.bfloat16
F32 = jnp.float32
MESH = pl.DeviceIdType.MESH

N = 16
FRAMES_OWN = 8
STEPS = 8
BB = 8


def filter_window():
    position = np.arange(TAPS * POINTS, dtype=np.float64)
    total = float(TAPS * POINTS)
    taper = 0.5 - 0.5 * np.cos(2.0 * np.pi / total * position)
    kernel = np.sinc((position - 0.5 * total) / POINTS) * taper
    return jnp.asarray(kernel.reshape(TAPS, CH_LO, CH_HI).astype(np.float32))


def dft_table(points):
    counter = np.arange(points)
    angles = 2.0 * np.pi / points * (counter[:, None] * counter[None, :] % points)
    cosine = np.cos(angles) / math.sqrt(points)
    sine = np.sin(angles) / math.sqrt(points)
    return np.stack([np.stack([cosine, sine]), np.stack([-sine, cosine])])


def low_matrix():
    table = dft_table(CH_LO)
    eye = np.eye(8)
    full = np.einsum("oqkn,fg->kofgqn", table, eye)
    return jnp.asarray(full.reshape(512, 512).astype(np.float32)).astype(BF)


def high_matrix():
    table = dft_table(CH_HI)
    return jnp.asarray(
        table.transpose(1, 2, 0, 3).reshape(256, 256).astype(np.float32)
    ).astype(BF)


def twiddle_table():
    angle = 2.0 * np.pi / POINTS * (np.arange(CH_LO)[:, None] * np.arange(CH_HI)[None, :])
    pair = np.stack([np.cos(angle), np.sin(angle)], axis=1)
    return jnp.asarray(np.concatenate([pair, pair], axis=-1).astype(np.float32))


def turn_parts(turns):
    t = (turns - jnp.round(turns)) * math.pi
    y = t * t
    s = t * (
        1.0
        + y
        * (
            -1.0 / 6
            + y
            * (
                1.0 / 120
                + y * (-1.0 / 5040 + y * (1.0 / 362880 + y * (-1.0 / 39916800 + y / 6227020800.0)))
            )
        )
    )
    c = 1.0 + y * (
        -0.5
        + y
        * (
            1.0 / 24
            + y
            * (
                -1.0 / 720
                + y * (1.0 / 40320 + y * (-1.0 / 3628800 + y * (1.0 / 479001600)))
            )
        )
    )
    return 1.0 - 2.0 * s * s, 2.0 * s * c


def z_shift(step):
    k = 7 - step
    half = (k + 1) // 2
    return half * (2 * (k % 2) - 1)


def fused(
    pointing, xv, win, low, high, twid, table, group,
    out,
    rbuf, filt, first, rotated, chan, recv, delay, weights, acc, csend,
    entered, send_a, recv_a, send_b, recv_b, send_c, recv_c,
):
    i = lax.axis_index("stn")
    j = lax.axis_index("tf")
    z = i // 2
    parity = j % 2

    barrier = pltpu.get_barrier_semaphore()

    def greet(step, carry):
        pl.semaphore_signal(
            barrier, inc=1, device_id=(i, lax.rem(j + step, N)), device_id_type=MESH
        )
        pl.semaphore_signal(
            barrier, inc=1, device_id=(lax.rem(i + step, N), j), device_id_type=MESH
        )
        return carry

    lax.fori_loop(1, N, greet, 0)

    frames_here = rbuf.at[:, pl.ds(16 + 8 * j, 8)]
    own_a = pltpu.make_async_copy(xv.at[:, j // 2, parity], frames_here, recv_a)
    own_a.start()
    pl.semaphore_wait(barrier, 2 * (N - 1))

    def send_voltages(step, carry):
        target = lax.rem(j + step, N)
        pltpu.make_async_remote_copy(
            src_ref=xv.at[:, target // 2, lax.rem(target, 2)],
            dst_ref=frames_here,
            send_sem=send_a,
            recv_sem=recv_a,
            device_id=(i, target),
            device_id_type=MESH,
        ).start()
        return carry

    lax.fori_loop(1, N, send_voltages, 0)

    def tell(step, carry):
        pl.semaphore_signal(
            entered, inc=1, device_id=(i, lax.rem(j + step, N)), device_id_type=MESH
        )
        return carry

    lax.fori_loop(1, N, tell, 0)

    rbuf[:, pl.ds(0, 16)] = jnp.zeros((2, 16, CH_LO, CH_HI), BF)
    acc[...] = jnp.zeros(acc.shape, F32)

    groups = group[...]
    for b in range(BB):
        row = jnp.zeros((1, CH_HI), F32)
        for g in range(GROUPS):
            row = jnp.where(groups == g, table[pl.ds(pointing[4 * b + g], 1), :], row)
        delay[pl.ds(b, 1), :] = row
    lane = lax.broadcasted_iota(jnp.int32, (8, CH_HI), 1)
    whose = jnp.broadcast_to(groups, (8, CH_HI))

    def make_weights(part, carry):
        for more in range(4):
            s = part * 4 + more
            here = lane == s
            column = jnp.sum(jnp.where(here, delay[...], 0.0), axis=1, keepdims=True)
            mine = jnp.sum(jnp.where(here, whose, 0), axis=1, keepdims=True)
            for k2 in range(2):
                channel = (2 * j + k2) + CH_LO * lane
                fraction = channel.astype(F32) * (1.0 / POINTS)
                cosine, sine = turn_parts(column * fraction)
                scale = math.sqrt(GROUPS / 128)
                cosine = (scale * cosine).astype(BF).astype(F32)
                sine = (-scale * sine).astype(BF).astype(F32)
                for g in range(GROUPS):
                    weights[s, k2, 0, pl.ds(8 * g, 8), :] = jnp.where(mine == g, cosine, 0.0)
                    weights[s, k2, 1, pl.ds(8 * g, 8), :] = jnp.where(mine == g, sine, 0.0)
        return carry

    lax.fori_loop(0, 32, make_weights, 0)
    pl.semaphore_wait(entered, N - 1)

    pltpu.make_async_copy(rbuf.at[:, pl.ds(16, 128)], rbuf.at[:, pl.ds(16, 128)], recv_a).wait()

    def block(step, carry):
        fb = lax.rem(z + z_shift(step) + 8, 8)
        i_to = 2 * fb + parity

        def filter_part(part, inner):
            q = part // 2
            row = pl.multiple_of((part % 2) * 16, 16)
            for g2 in range(2):
                base = fb * 16 + g2 * 8
                sums = [None] * 8
                taps = [win[t, pl.ds(row, 16), :] for t in range(TAPS)]
                for k in range(1, 24):
                    x = rbuf[q, base + k, pl.ds(row, 16), :].astype(F32)
                    for f in range(8):
                        t = k - 1 - f
                        if 0 <= t < TAPS:
                            term = taps[t] * x
                            sums[f] = term if sums[f] is None else sums[f] + term
                for f in range(8):
                    filt[pl.ds(pl.multiple_of(f * 64 + q * 32 + row, 16), 16), pl.ds(128 * g2, 128)] = sums[f].astype(BF)
            return inner

        lax.fori_loop(0, 4, filter_part, 0)

        first[...] = jnp.dot(low[...], filt[...], preferred_element_type=F32).reshape(32, 2, 8, 256)

        def turn(c, inner):
            part = pl.ds(c * 8, 8)
            real, imag = first[part, 0], first[part, 1]
            cosine, sine = twid[part, 0:1, :], twid[part, 1:2, :]
            re = real * cosine + imag * sine
            im = imag * cosine - real * sine
            re = jnp.concatenate([re[:, :, :128], re[:, :, 128:]], axis=1).astype(BF)
            im = jnp.concatenate([im[:, :, :128], im[:, :, 128:]], axis=1).astype(BF)
            rotated[part] = jnp.concatenate([re, im], axis=2)
            return inner

        lax.fori_loop(0, 4, turn, 0)
        done = jnp.dot(rotated[...].reshape(512, 256), high[...], preferred_element_type=F32)
        chan[step] = done.astype(BF).reshape(CH_LO, 16, 256)

        def send(n, inner):
            j_to = lax.rem(j + n, N)
            here = jnp.logical_and(i_to == i, j_to == j)
            source = chan.at[step, pl.ds(2 * j_to, 2)]
            target = recv.at[8 * i + j // 2]

            @pl.when(here)
            def _():
                pltpu.make_async_copy(source, target, recv_b.at[i]).start()

            @pl.when(jnp.logical_not(here))
            def _():
                pltpu.make_async_remote_copy(
                    src_ref=source,
                    dst_ref=target,
                    send_sem=send_b.at[step],
                    recv_sem=recv_b.at[i],
                    device_id=(i_to, j_to),
                    device_id_type=MESH,
                ).start()

            return inner

        lax.fori_loop(0, N, send, 0)
        return carry

    lax.fori_loop(0, STEPS, block, 0)

    def add_block(step, carry):
        z_from = lax.rem(z - z_shift(step // 2) + 8, 8)
        i_from = 2 * z_from + step % 2
        s0 = 8 * i_from
        pltpu.make_async_copy(recv.at[pl.ds(s0, 8)], recv.at[pl.ds(s0, 8)], recv_b.at[i_from]).wait()

        def part(n, inner):
            k2 = n // 4
            g = n % 4
            re = [acc[k2, g, b, 0] for b in range(BB)]
            im = [acc[k2, g, b, 1] for b in range(BB)]
            for s in range(8):
                value = recv[s0 + s, k2].astype(F32)
                vr, vi = value[:, :128], value[:, 128:]
                for b in range(BB):
                    wr = weights[s0 + s, k2, 0, pl.ds(8 * g + b, 1), :]
                    wi = weights[s0 + s, k2, 1, pl.ds(8 * g + b, 1), :]
                    re[b] = re[b] + (wr * vr - wi * vi)
                    im[b] = im[b] + (wr * vi + wi * vr)
            for b in range(BB):
                acc[k2, g, b, 0] = re[b]
                acc[k2, g, b, 1] = im[b]
            return inner

        lax.fori_loop(0, 8, part, 0)
        return carry

    lax.fori_loop(0, N, add_block, 0)

    for k2 in range(2):
        for g in range(GROUPS):
            for b in range(BB):
                for q in range(2):
                    csend[2 * b + g // 2, g % 2, q, k2] = acc[k2, g, b, q].astype(BF)

    own_c = pltpu.make_async_copy(csend.at[i], out.at[i], recv_c)
    own_c.start()

    def send_beams(step, carry):
        target = lax.rem(i + step, N)
        pltpu.make_async_remote_copy(
            src_ref=csend.at[target],
            dst_ref=out.at[i],
            send_sem=send_c,
            recv_sem=recv_c,
            device_id=(target, j),
            device_id_type=MESH,
        ).start()
        return carry

    lax.fori_loop(1, N, send_beams, 0)

    pltpu.make_async_copy(rbuf.at[:, pl.ds(0, 120)], rbuf.at[:, pl.ds(0, 120)], send_a).wait()

    def wait_sent(step, carry):
        fb = lax.rem(z + z_shift(step) + 8, 8)
        mine = 2 * fb + parity == i

        @pl.when(mine)
        def _():
            pltpu.make_async_copy(
                chan.at[step, pl.ds(0, 30)], chan.at[step, pl.ds(0, 30)], send_b.at[step]
            ).wait()

        @pl.when(jnp.logical_not(mine))
        def _():
            pltpu.make_async_copy(chan.at[step], chan.at[step], send_b.at[step]).wait()

        return carry

    lax.fori_loop(0, STEPS, wait_sent, 0)
    pltpu.make_async_copy(csend.at[pl.ds(0, 15)], csend.at[pl.ds(0, 15)], send_c).wait()
    pltpu.make_async_copy(csend, csend, recv_c).wait()


def body(voltages, delay_table, beam_pointing, station_group):
    stations_here = voltages.shape[1]
    xv = voltages.reshape(2, stations_here, 2, FRAMES_OWN, CH_LO, CH_HI)

    vmem = pl.BlockSpec(memory_space=pltpu.VMEM)
    anywhere = pl.BlockSpec(memory_space=pl.ANY)
    out = pl.pallas_call(
        fused,
        out_shape=jax.ShapeDtypeStruct((N, 2, 2, 2, 16, CH_HI), BF),
        in_specs=[pl.BlockSpec(memory_space=pltpu.SMEM), anywhere] + [vmem] * 6,
        out_specs=anywhere,
        scratch_shapes=[
            pltpu.VMEM((2, 144, CH_LO, CH_HI), BF),
            pltpu.VMEM((512, 256), BF),
            pltpu.VMEM((CH_LO, 2, 8, 256), F32),
            pltpu.VMEM((CH_LO, 16, 256), BF),
            pltpu.VMEM((STEPS, CH_LO, 16, 256), BF),
            pltpu.VMEM((128, 2, 16, 256), BF),
            pltpu.VMEM((8, 128), F32),
            pltpu.VMEM((128, 2, 2, 32, CH_HI), F32),
            pltpu.VMEM((2, GROUPS, BB, 2, 16, CH_HI), F32),
            pltpu.VMEM((N, 2, 2, 2, 16, CH_HI), BF),
            pltpu.SemaphoreType.REGULAR,
            pltpu.SemaphoreType.DMA,
            pltpu.SemaphoreType.DMA,
            pltpu.SemaphoreType.DMA((STEPS,)),
            pltpu.SemaphoreType.DMA((N,)),
            pltpu.SemaphoreType.DMA,
            pltpu.SemaphoreType.DMA,
        ],
        compiler_params=pltpu.CompilerParams(
            has_side_effects=True, collective_id=0, vmem_limit_bytes=40 * 1024 * 1024
        ),
        name="channelize_and_beamform",
    )(
        beam_pointing, xv, filter_window(), low_matrix(), high_matrix(), twiddle_table(),
        delay_table, station_group.reshape(1, -1),
    )

    out = out.reshape(8, 2, 2, 2, 2, 16, CH_HI).transpose(2, 3, 1, 0, 5, 4, 6)
    return out.reshape(2, 2, 2, 128, 2, CH_HI)


def solution(mesh):
    in_specs = (P(None, "stn", None, "tf"), P(), P(), P())
    out_specs = P("stn", None, None, None, "tf", None)
    return jax.shard_map(body, mesh=mesh, in_specs=in_specs, out_specs=out_specs, check_vma=False)
```

```python
import math

import jax
import jax.numpy as jnp
import numpy as np
from jax import lax
from jax.experimental import pallas as pl
from jax.experimental.pallas import tpu as pltpu
from jax.sharding import PartitionSpec as P

TAPS = 16
CH_LO = 32
CH_HI = 128
POINTS = CH_LO * CH_HI
GROUPS = 4
TWO_PI = 2.0 * math.pi
BF = jnp.bfloat16
F32 = jnp.float32
MESH = pl.DeviceIdType.MESH

N = 16
FRAMES_OWN = 8
STEPS = 8
BB = 8


def filter_window():
    position = np.arange(TAPS * POINTS, dtype=np.float64)
    total = float(TAPS * POINTS)
    taper = 0.5 - 0.5 * np.cos(2.0 * np.pi / total * position)
    kernel = np.sinc((position - 0.5 * total) / POINTS) * taper
    return jnp.asarray(kernel.reshape(TAPS, CH_LO, CH_HI).astype(np.float32))


def dft_table(points):
    counter = np.arange(points)
    angles = 2.0 * np.pi / points * (counter[:, None] * counter[None, :] % points)
    cosine = np.cos(angles) / math.sqrt(points)
    sine = np.sin(angles) / math.sqrt(points)
    return np.stack([np.stack([cosine, sine]), np.stack([-sine, cosine])])


def low_matrix():
    table = dft_table(CH_LO)
    eye = np.eye(8)
    full = np.einsum("oqkn,fg->kofgqn", table, eye)
    return jnp.asarray(full.reshape(512, 512).astype(np.float32)).astype(BF)


def high_matrix():
    table = dft_table(CH_HI)
    return jnp.asarray(
        table.transpose(1, 2, 0, 3).reshape(256, 256).astype(np.float32)
    ).astype(BF)


def twiddle_table():
    angle = 2.0 * np.pi / POINTS * (np.arange(CH_LO)[:, None] * np.arange(CH_HI)[None, :])
    pair = np.stack([np.cos(angle), np.sin(angle)], axis=1)
    return jnp.asarray(np.concatenate([pair, pair], axis=-1).astype(np.float32))


def turn_parts(turns):
    t = (turns - jnp.round(turns)) * math.pi
    y = t * t
    s = t * (
        1.0
        + y
        * (
            -1.0 / 6
            + y
            * (
                1.0 / 120
                + y * (-1.0 / 5040 + y * (1.0 / 362880 + y * (-1.0 / 39916800 + y / 6227020800.0)))
            )
        )
    )
    c = 1.0 + y * (
        -0.5
        + y
        * (
            1.0 / 24
            + y
            * (
                -1.0 / 720
                + y * (1.0 / 40320 + y * (-1.0 / 3628800 + y * (1.0 / 479001600)))
            )
        )
    )
    return 1.0 - 2.0 * s * s, 2.0 * s * c


def turn_of(step):
    return lax.rem(2 + 3 * step, 4)


def fused(
    pointing, xv, win, low, high, twid, table, group,
    out,
    rbuf, filt, first, rotated, chan, recv, delay, weights, acc, csend,
    entered, send_a, recv_a, send_r, recv_r, send_b, recv_b, send_c, recv_c,
):
    i = lax.axis_index("stn")
    j = lax.axis_index("tf")
    z, xh = i // 2, lax.rem(i, 2)
    station, half = j // 2, lax.rem(j, 2)
    own_half = j // 8
    keeps = own_half == half

    barrier = pltpu.get_barrier_semaphore()

    def greet(step, carry):
        pl.semaphore_signal(
            barrier, inc=1, device_id=(i, lax.rem(j + step, N)), device_id_type=MESH
        )
        pl.semaphore_signal(
            barrier, inc=1, device_id=(lax.rem(i + step, N), j), device_id_type=MESH
        )
        return carry

    lax.fori_loop(1, N, greet, 0)
    pl.semaphore_wait(barrier, 2 * (N - 1))

    def send_voltages(p):
        block = pl.ds(16 + 8 * lax.rem(j, 8), 8)

        def send(step, carry):
            s_to = lax.rem(station + step, 8)
            j_to = 2 * s_to + own_half

            @pl.when(j_to == j)
            def _():
                pltpu.make_async_copy(xv.at[:, s_to, p], rbuf.at[p, :, block], recv_a.at[p]).start()

            @pl.when(j_to != j)
            def _():
                pltpu.make_async_remote_copy(
                    src_ref=xv.at[:, s_to, p],
                    dst_ref=rbuf.at[p, :, block],
                    send_sem=send_a.at[p],
                    recv_sem=recv_a.at[p],
                    device_id=(i, j_to),
                    device_id_type=MESH,
                ).start()

            return carry

        lax.fori_loop(0, 8, send, 0)

    def wait_voltages_sent(p):
        @pl.when(keeps)
        def _():
            part = rbuf.at[p, :, pl.ds(0, 56)]
            pltpu.make_async_copy(part, part, send_a.at[p]).wait()

        @pl.when(jnp.logical_not(keeps))
        def _():
            part = rbuf.at[p, :, pl.ds(0, 64)]
            pltpu.make_async_copy(part, part, send_a.at[p]).wait()

    def relay(p):
        return pltpu.make_async_remote_copy(
            src_ref=rbuf.at[p, :, pl.ds(64, 16)],
            dst_ref=rbuf.at[p, :, pl.ds(0, 16)],
            send_sem=send_r.at[p],
            recv_sem=recv_r.at[p],
            device_id=(i, j + 1),
            device_id_type=MESH,
        )

    def take_voltages(p):
        part = rbuf.at[p, :, pl.ds(16, 64)]
        pltpu.make_async_copy(part, part, recv_a.at[p]).wait()

        @pl.when(half == 0)
        def _():
            relay(p).start()

        @pl.when(half == 1)
        def _():
            part = rbuf.at[p, :, pl.ds(0, 16)]
            pltpu.make_async_copy(part, part, recv_r.at[p]).wait()

    send_voltages(0)

    def tell(step, carry):
        pl.semaphore_signal(
            entered, inc=1, device_id=(i, lax.rem(j + step, N)), device_id_type=MESH
        )
        return carry

    lax.fori_loop(1, N, tell, 0)

    @pl.when(half == 0)
    def _():
        rbuf[:, :, pl.ds(0, 16)] = jnp.zeros((2, 2, 16, CH_LO, CH_HI), BF)

    groups = group[...]
    for b in range(BB):
        row = jnp.zeros((1, CH_HI), F32)
        for g in range(GROUPS):
            row = jnp.where(groups == g, table[pl.ds(pointing[4 * b + g], 1), :], row)
        delay[pl.ds(b, 1), :] = row
    lane = lax.broadcasted_iota(jnp.int32, (8, CH_HI), 1)
    whose = jnp.broadcast_to(groups, (8, CH_HI))

    def make_weights(part, carry):
        for more in range(4):
            s = part * 4 + more
            here = lane == s
            column = jnp.sum(jnp.where(here, delay[...], 0.0), axis=1, keepdims=True)
            mine = jnp.sum(jnp.where(here, whose, 0), axis=1, keepdims=True)
            for k2 in range(2):
                channel = (2 * j + k2) + CH_LO * lane
                fraction = channel.astype(F32) * (1.0 / POINTS)
                cosine, sine = turn_parts(column * fraction)
                scale = math.sqrt(GROUPS / 128)
                cosine = (scale * cosine).astype(BF).astype(F32)
                sine = (-scale * sine).astype(BF).astype(F32)
                for g in range(GROUPS):
                    weights[s, k2, 0, pl.ds(8 * g, 8), :] = jnp.where(mine == g, cosine, 0.0)
                    weights[s, k2, 1, pl.ds(8 * g, 8), :] = jnp.where(mine == g, sine, 0.0)
        return carry

    lax.fori_loop(0, 32, make_weights, 0)
    wait_voltages_sent(0)
    send_voltages(1)
    pl.semaphore_wait(entered, N - 1)

    def block(p, step):
        at = 4 * p + step
        near = lax.rem(z + turn_of(step), 4)
        fb = 4 * half + near

        def filter_part(part, inner):
            q = part // 2
            row = pl.multiple_of((part % 2) * 16, 16)
            for g2 in range(2):
                base = near * 16 + g2 * 8
                sums = [None] * 8
                taps = [win[t, pl.ds(row, 16), :] for t in range(TAPS)]
                for k in range(1, 24):
                    x = rbuf[p, q, base + k, pl.ds(row, 16), :].astype(F32)
                    for f in range(8):
                        t = k - 1 - f
                        if 0 <= t < TAPS:
                            term = taps[t] * x
                            sums[f] = term if sums[f] is None else sums[f] + term
                for f in range(8):
                    to = pl.ds(pl.multiple_of(f * 64 + q * 32 + row, 16), 16)
                    filt[to, pl.ds(128 * g2, 128)] = sums[f].astype(BF)
            return inner

        lax.fori_loop(0, 4, filter_part, 0)

        first[...] = jnp.dot(low[...], filt[...], preferred_element_type=F32).reshape(32, 2, 8, 256)

        def turn(c, inner):
            part = pl.ds(c * 8, 8)
            real, imag = first[part, 0], first[part, 1]
            cosine, sine = twid[part, 0:1, :], twid[part, 1:2, :]
            re = real * cosine + imag * sine
            im = imag * cosine - real * sine
            for g2 in range(2):
                lanes = slice(128 * g2, 128 * g2 + 128)
                both = jnp.concatenate([re[:, :, lanes], im[:, :, lanes]], axis=2).reshape(64, 256)
                rotated[pl.ds(pl.multiple_of(256 * g2 + 64 * c, 64), 64), :] = both.astype(BF)
            return inner

        lax.fori_loop(0, 4, turn, 0)
        done = jnp.dot(rotated[...], high[...], preferred_element_type=F32)
        chan[at] = done.astype(BF).reshape(2 * N, 16, 256)

        def send(n, inner):
            j_to = lax.rem(j + n, N)
            for g2 in range(2):
                here = jnp.logical_and(2 * fb + g2 == i, j_to == j)
                source = chan.at[at, N * g2 + j_to]
                target = recv.at[p, 8 * i + station]

                @pl.when(here)
                def _():
                    pltpu.make_async_copy(source, target, recv_b.at[p, i]).start()

                @pl.when(jnp.logical_not(here))
                def _():
                    pltpu.make_async_remote_copy(
                        src_ref=source,
                        dst_ref=target,
                        send_sem=send_b.at[at],
                        recv_sem=recv_b.at[p, i],
                        device_id=(2 * fb + g2, j_to),
                        device_id_type=MESH,
                    ).start()

            return inner

        lax.fori_loop(0, N, send, 0)

    def blocks(n, carry):
        p = n // 4

        @pl.when(lax.rem(n, 4) == 0)
        def _():
            take_voltages(p)

        block(p, lax.rem(n, 4))
        return carry

    lax.fori_loop(0, 8, blocks, 0)

    def add_block(p, step, last):
        z_from = lax.rem(z - turn_of(step // 4) + 8, 4) + 4 * lax.rem(step // 2, 2)
        i_from = 2 * z_from + lax.rem(step, 2)
        s0 = 8 * i_from
        part = recv.at[p, pl.ds(s0, 8)]
        pltpu.make_async_copy(part, part, recv_b.at[p, i_from]).wait()

        def some(g, inner):
            sums = [[[acc[g, b, q, k2] for k2 in range(2)] for q in range(2)] for b in range(BB)]
            for s in range(8):
                value = recv[p, s0 + s].astype(F32)
                for k2 in range(2):
                    vr = value[8 * k2 : 8 * k2 + 8, :128]
                    vi = value[8 * k2 : 8 * k2 + 8, 128:]
                    for b in range(BB):
                        wr = weights[s0 + s, k2, 0, pl.ds(8 * g + b, 1), :]
                        wi = weights[s0 + s, k2, 1, pl.ds(8 * g + b, 1), :]
                        sums[b][0][k2] = sums[b][0][k2] + (wr * vr - wi * vi)
                        sums[b][1][k2] = sums[b][1][k2] + (wr * vi + wi * vr)
            for b in range(BB):
                for q in range(2):
                    if last:
                        both = jnp.concatenate(sums[b][q], axis=0).astype(BF)
                        csend[p, 2 * b + g // 2, lax.rem(g, 2), q] = both
                    else:
                        for k2 in range(2):
                            acc[g, b, q, k2] = sums[b][q][k2]
            return inner

        lax.fori_loop(0, GROUPS, some, 0)

    def beams(p, carry):
        acc[...] = jnp.zeros(acc.shape, F32)

        def add_early(step, inner):
            add_block(p, step, False)
            return inner

        lax.fori_loop(0, N - 1, add_early, 0)
        add_block(p, jnp.int32(N - 1), True)
        pltpu.make_async_copy(csend.at[p, i], out.at[p, i], recv_c.at[p]).start()

        def send_beams(step, inner):
            target = lax.rem(i + step, N)
            pltpu.make_async_remote_copy(
                src_ref=csend.at[p, target],
                dst_ref=out.at[p, i],
                send_sem=send_c.at[p],
                recv_sem=recv_c.at[p],
                device_id=(target, j),
                device_id_type=MESH,
            ).start()
            return inner

        lax.fori_loop(1, N, send_beams, 0)
        return carry

    lax.fori_loop(0, 2, beams, 0)

    wait_voltages_sent(1)

    @pl.when(half == 0)
    def _():
        for p in range(2):
            relay(p).wait_send()

    def wait_sent(at, carry):
        fb = 4 * half + lax.rem(z + turn_of(lax.rem(at, 4)), 4)
        mine = fb == z

        @pl.when(mine)
        def _():
            part = chan.at[at, pl.ds(0, 2 * N - 1)]
            pltpu.make_async_copy(part, part, send_b.at[at]).wait()

        @pl.when(jnp.logical_not(mine))
        def _():
            pltpu.make_async_copy(chan.at[at], chan.at[at], send_b.at[at]).wait()

        return carry

    lax.fori_loop(0, STEPS, wait_sent, 0)
    for p in range(2):
        part = csend.at[p, pl.ds(0, N - 1)]
        pltpu.make_async_copy(part, part, send_c.at[p]).wait()
        pltpu.make_async_copy(csend.at[p], csend.at[p], recv_c.at[p]).wait()


def body(voltages, delay_table, beam_pointing, station_group):
    stations_here = voltages.shape[1]
    xv = voltages.reshape(2, stations_here, 2, FRAMES_OWN, CH_LO, CH_HI)

    vmem = pl.BlockSpec(memory_space=pltpu.VMEM)
    anywhere = pl.BlockSpec(memory_space=pl.ANY)
    out = pl.pallas_call(
        fused,
        out_shape=jax.ShapeDtypeStruct((2, N, 2, 2, 16, CH_HI), BF),
        in_specs=[pl.BlockSpec(memory_space=pltpu.SMEM), anywhere] + [vmem] * 6,
        out_specs=anywhere,
        scratch_shapes=[
            pltpu.VMEM((2, 2, 80, CH_LO, CH_HI), BF),
            pltpu.VMEM((512, 256), BF),
            pltpu.VMEM((CH_LO, 2, 8, 256), F32),
            pltpu.VMEM((512, 256), BF),
            pltpu.VMEM((STEPS, 2 * N, 16, 256), BF),
            pltpu.VMEM((2, 128, 16, 256), BF),
            pltpu.VMEM((8, 128), F32),
            pltpu.VMEM((128, 2, 2, 32, CH_HI), F32),
            pltpu.VMEM((GROUPS, BB, 2, 2, 8, CH_HI), F32),
            pltpu.VMEM((2, N, 2, 2, 16, CH_HI), BF),
            pltpu.SemaphoreType.REGULAR,
            pltpu.SemaphoreType.DMA((2,)),
            pltpu.SemaphoreType.DMA((2,)),
            pltpu.SemaphoreType.DMA((2,)),
            pltpu.SemaphoreType.DMA((2,)),
            pltpu.SemaphoreType.DMA((STEPS,)),
            pltpu.SemaphoreType.DMA((2, N)),
            pltpu.SemaphoreType.DMA((2,)),
            pltpu.SemaphoreType.DMA((2,)),
        ],
        compiler_params=pltpu.CompilerParams(
            has_side_effects=True, collective_id=0, vmem_limit_bytes=40 * 1024 * 1024
        ),
        name="channelize_and_beamform",
    )(
        beam_pointing, xv, filter_window(), low_matrix(), high_matrix(), twiddle_table(),
        delay_table, station_group.reshape(1, -1),
    )

    out = out.reshape(2, N, 2, 2, 2, 8, CH_HI).transpose(2, 3, 0, 1, 5, 4, 6)
    return out.reshape(2, 2, 2, 128, 2, CH_HI)


def solution(mesh):
    in_specs = (P(None, "stn", None, "tf"), P(), P(), P())
    out_specs = P("stn", None, None, None, "tf", None)
    return jax.shard_map(body, mesh=mesh, in_specs=in_specs, out_specs=out_specs, check_vma=False)
```

```python
import math

import jax
import jax.numpy as jnp
import numpy as np
from jax import lax
from jax.experimental import pallas as pl
from jax.experimental.pallas import tpu as pltpu
from jax.sharding import PartitionSpec as P

TAPS = 16
CH_LO = 32
CH_HI = 128
POINTS = CH_LO * CH_HI
GROUPS = 4
TWO_PI = 2.0 * math.pi
BF = jnp.bfloat16
F32 = jnp.float32
MESH = pl.DeviceIdType.MESH

N = 16
FRAMES_OWN = 8
STEPS = 8
BB = 8


def filter_window():
    position = np.arange(TAPS * POINTS, dtype=np.float64)
    total = float(TAPS * POINTS)
    taper = 0.5 - 0.5 * np.cos(2.0 * np.pi / total * position)
    kernel = np.sinc((position - 0.5 * total) / POINTS) * taper
    return jnp.asarray(kernel.reshape(TAPS, CH_LO, CH_HI).astype(np.float32))


def dft_table(points):
    counter = np.arange(points)
    angles = 2.0 * np.pi / points * (counter[:, None] * counter[None, :] % points)
    cosine = np.cos(angles) / math.sqrt(points)
    sine = np.sin(angles) / math.sqrt(points)
    return np.stack([np.stack([cosine, sine]), np.stack([-sine, cosine])])


def low_matrix():
    table = dft_table(CH_LO)
    eye = np.eye(8)
    full = np.einsum("oqkn,fg->kofgqn", table, eye)
    return jnp.asarray(full.reshape(512, 512).astype(np.float32)).astype(BF)


def high_matrix():
    table = dft_table(CH_HI)
    return jnp.asarray(
        table.transpose(1, 2, 0, 3).reshape(256, 256).astype(np.float32)
    ).astype(BF)


def twiddle_table():
    angle = 2.0 * np.pi / POINTS * (np.arange(CH_LO)[:, None] * np.arange(CH_HI)[None, :])
    pair = np.stack([np.cos(angle), np.sin(angle)], axis=1)
    return jnp.asarray(np.concatenate([pair, pair], axis=-1).astype(np.float32))


def turn_parts(turns):
    t = (turns - jnp.round(turns)) * math.pi
    y = t * t
    s = t * (
        1.0
        + y
        * (
            -1.0 / 6
            + y
            * (
                1.0 / 120
                + y * (-1.0 / 5040 + y * (1.0 / 362880 + y * (-1.0 / 39916800 + y / 6227020800.0)))
            )
        )
    )
    c = 1.0 + y * (
        -0.5
        + y
        * (
            1.0 / 24
            + y
            * (
                -1.0 / 720
                + y * (1.0 / 40320 + y * (-1.0 / 3628800 + y * (1.0 / 479001600)))
            )
        )
    )
    return 1.0 - 2.0 * s * s, 2.0 * s * c


def turn_of(step):
    return lax.rem(2 + 3 * step, 4)


def fused(
    pointing, xv, win, low, high, twid, table, group,
    out,
    rbuf, filt, first, rotated, chan, recv_0, recv_1, delay, weights, order, running, csend,
    order_smem, order_sem, entered, send_a, recv_a, send_r, recv_r, send_b, recv_b, send_c, recv_c,
):
    i = lax.axis_index("stn")
    j = lax.axis_index("tf")
    z = i // 2
    recv = (recv_0, recv_1)
    station, half = j // 2, lax.rem(j, 2)
    own_half = j // 8
    keeps = own_half == half

    barrier = pltpu.get_barrier_semaphore()

    def greet(step, carry):
        pl.semaphore_signal(
            barrier, inc=1, device_id=(i, lax.rem(j + step, N)), device_id_type=MESH
        )
        pl.semaphore_signal(
            barrier, inc=1, device_id=(lax.rem(i + step, N), j), device_id_type=MESH
        )
        return carry

    lax.fori_loop(1, N, greet, 0)
    pl.semaphore_wait(barrier, 2 * (N - 1))

    def send_voltages(p):
        block = pl.ds(16 + 8 * lax.rem(j, 8), 8)

        def send(step, carry):
            s_to = lax.rem(station + step, 8)
            j_to = 2 * s_to + own_half

            @pl.when(j_to == j)
            def _():
                pltpu.make_async_copy(xv.at[:, s_to, p], rbuf.at[p, :, block], recv_a.at[p]).start()

            @pl.when(j_to != j)
            def _():
                pltpu.make_async_remote_copy(
                    src_ref=xv.at[:, s_to, p],
                    dst_ref=rbuf.at[p, :, block],
                    send_sem=send_a.at[p],
                    recv_sem=recv_a.at[p],
                    device_id=(i, j_to),
                    device_id_type=MESH,
                ).start()

            return carry

        lax.fori_loop(0, 8, send, 0)

    def wait_voltages_sent(p):
        @pl.when(keeps)
        def _():
            part = rbuf.at[p, :, pl.ds(0, 56)]
            pltpu.make_async_copy(part, part, send_a.at[p]).wait()

        @pl.when(jnp.logical_not(keeps))
        def _():
            part = rbuf.at[p, :, pl.ds(0, 64)]
            pltpu.make_async_copy(part, part, send_a.at[p]).wait()

    def relay(p):
        return pltpu.make_async_remote_copy(
            src_ref=rbuf.at[p, :, pl.ds(64, 16)],
            dst_ref=rbuf.at[p, :, pl.ds(0, 16)],
            send_sem=send_r.at[p],
            recv_sem=recv_r.at[p],
            device_id=(i, j + 1),
            device_id_type=MESH,
        )

    def take_voltages(p):
        part = rbuf.at[p, :, pl.ds(16, 64)]
        pltpu.make_async_copy(part, part, recv_a.at[p]).wait()

        @pl.when(half == 0)
        def _():
            relay(p).start()

    send_voltages(0)

    def tell(step, carry):
        pl.semaphore_signal(
            entered, inc=1, device_id=(i, lax.rem(j + step, N)), device_id_type=MESH
        )
        return carry

    lax.fori_loop(1, N, tell, 0)

    @pl.when(half == 0)
    def _():
        rbuf[:, :, pl.ds(0, 16)] = jnp.zeros((2, 2, 16, CH_LO, CH_HI), BF)

    groups = group[...]
    for b in range(BB):
        row = jnp.zeros((1, CH_HI), F32)
        for g in range(GROUPS):
            row = jnp.where(groups == g, table[pl.ds(pointing[4 * b + g], 1), :], row)
        delay[pl.ds(b, 1), :] = row
    lane = lax.broadcasted_iota(jnp.int32, (8, CH_HI), 1)

    wide = jnp.broadcast_to(groups, (128, CH_HI))
    lanes = lax.broadcasted_iota(jnp.int32, (128, CH_HI), 1)
    rows = lax.broadcasted_iota(jnp.int32, (128, CH_HI), 0)
    own = jnp.sum(jnp.where(rows == lanes, wide, 0), axis=1, keepdims=True)
    ahead = jnp.logical_or(wide < own, jnp.logical_and(wide == own, lanes < rows))
    place = jnp.sum(jnp.where(ahead, 1, 0), axis=1, keepdims=True)
    starts = jnp.sum(jnp.where(own < lanes, 1, 0), axis=0, keepdims=True)
    opens = jnp.zeros((1, CH_HI), jnp.int32)
    for g in range(GROUPS):
        opens = jnp.where(starts[:, g : g + 1] == lanes[:1], 1, opens)
    order[...] = jnp.zeros((8, CH_HI), jnp.int32)
    order[pl.ds(0, 1), :] = jnp.sum(jnp.where(place == lanes, rows, 0), axis=0, keepdims=True)
    order[pl.ds(1, 1), :] = opens
    order[pl.ds(2, 1), :] = starts
    order[pl.ds(3, 1), :] = jnp.sum(jnp.where(own <= lanes, 1, 0), axis=0, keepdims=True)
    order_copy = pltpu.make_async_copy(order, order_smem, order_sem)
    order_copy.start()

    def make_weights(part, carry):
        for more in range(4):
            s = part * 4 + more
            here = lane == s
            column = jnp.sum(jnp.where(here, delay[...], 0.0), axis=1, keepdims=True)
            for k2 in range(2):
                channel = (2 * j + k2) + CH_LO * lane
                fraction = channel.astype(F32) * (1.0 / POINTS)
                cosine, sine = turn_parts(column * fraction)
                scale = math.sqrt(GROUPS / 128)
                weights[s, k2, 0] = (scale * cosine).astype(BF).astype(F32)
                weights[s, k2, 1] = (-scale * sine).astype(BF).astype(F32)
        return carry

    lax.fori_loop(0, 32, make_weights, 0)
    order_copy.wait()
    wait_voltages_sent(0)
    send_voltages(1)
    pl.semaphore_wait(entered, N - 1)

    def block(p, step):
        at = 4 * p + step
        near = lax.rem(z + turn_of(step), 4)

        @pl.when(jnp.logical_and(half == 1, near == 0))
        def _():
            part = rbuf.at[p, :, pl.ds(0, 16)]
            pltpu.make_async_copy(part, part, recv_r.at[p]).wait()

        fb = 4 * half + near

        def filter_part(part, inner):
            q = part // 2
            row = pl.multiple_of((part % 2) * 16, 16)
            for g2 in range(2):
                base = near * 16 + g2 * 8
                sums = [None] * 8
                taps = [win[t, pl.ds(row, 16), :] for t in range(TAPS)]
                for k in range(1, 24):
                    x = rbuf[p, q, base + k, pl.ds(row, 16), :].astype(F32)
                    for f in range(8):
                        t = k - 1 - f
                        if 0 <= t < TAPS:
                            term = taps[t] * x
                            sums[f] = term if sums[f] is None else sums[f] + term
                for f in range(8):
                    to = pl.ds(pl.multiple_of(f * 64 + q * 32 + row, 16), 16)
                    filt[to, pl.ds(128 * g2, 128)] = sums[f].astype(BF)
            return inner

        lax.fori_loop(0, 4, filter_part, 0)

        first[...] = jnp.dot(low[...], filt[...], preferred_element_type=F32).reshape(32, 2, 8, 256)

        def turn(c, inner):
            part = pl.ds(c * 8, 8)
            real, imag = first[part, 0], first[part, 1]
            cosine, sine = twid[part, 0:1, :], twid[part, 1:2, :]
            re = real * cosine + imag * sine
            im = imag * cosine - real * sine
            for g2 in range(2):
                lanes = slice(128 * g2, 128 * g2 + 128)
                both = jnp.concatenate([re[:, :, lanes], im[:, :, lanes]], axis=2).reshape(64, 256)
                rotated[pl.ds(pl.multiple_of(256 * g2 + 64 * c, 64), 64), :] = both.astype(BF)
            return inner

        lax.fori_loop(0, 4, turn, 0)
        done = jnp.dot(rotated[...], high[...], preferred_element_type=F32)
        chan[at] = done.astype(BF).reshape(2 * N, 16, 256)

        def send(n, inner):
            j_to = lax.rem(j + n, N)
            for g2 in range(2):
                here = jnp.logical_and(2 * fb + g2 == i, j_to == j)
                source = chan.at[at, N * g2 + j_to]
                target = recv[p].at[8 * i + station]

                @pl.when(here)
                def _():
                    pltpu.make_async_copy(source, target, recv_b.at[p, i]).start()

                @pl.when(jnp.logical_not(here))
                def _():
                    pltpu.make_async_remote_copy(
                        src_ref=source,
                        dst_ref=target,
                        send_sem=send_b.at[at],
                        recv_sem=recv_b.at[p, i],
                        device_id=(2 * fb + g2, j_to),
                        device_id_type=MESH,
                    ).start()

            return inner

        lax.fori_loop(0, N, send, 0)

    for p in range(2):
        take_voltages(p)

        def blocks(step, carry, p=p):
            block(p, step)
            return carry

        lax.fori_loop(0, 4, blocks, 0)

    def beams(p):
        def arrive(i_from, carry):
            part = recv[p].at[pl.ds(8 * i_from, 8)]
            pltpu.make_async_copy(part, part, recv_b.at[p, i_from]).wait()
            return carry

        lax.fori_loop(0, N, arrive, 0)

        def add(m, sums):
            s = order_smem[0, m]
            keep = jnp.where(order_smem[1, m] > 0, 0.0, 1.0)
            value = recv[p][s].astype(F32)
            result = []
            for k2 in range(2):
                vr = value[8 * k2 : 8 * k2 + 8, :128]
                vi = value[8 * k2 : 8 * k2 + 8, 128:]
                for b in range(BB):
                    wr = weights[s, k2, 0, pl.ds(b, 1), :]
                    wi = weights[s, k2, 1, pl.ds(b, 1), :]
                    re, im = sums[2 * (BB * k2 + b)], sums[2 * (BB * k2 + b) + 1]
                    re = keep * re + (wr * vr - wi * vi)
                    im = keep * im + (wr * vi + wi * vr)
                    running[m, b, 0, k2] = re
                    running[m, b, 1, k2] = im
                    result += [re, im]
            return tuple(result)

        zero = jnp.zeros((8, CH_HI), F32)

        def add_some(part, sums):
            for more in range(2):
                sums = add(part * 2 + more, sums)
            return sums

        lax.fori_loop(0, 128 // 2, add_some, (zero,) * (4 * BB))

        def finish(g, carry):
            start, stop = order_smem[2, g], order_smem[3, g]
            some = jnp.where(stop > start, 1.0, 0.0)
            at = jnp.maximum(stop - 1, 0)
            for b in range(BB):
                for q in range(2):
                    total = some * running[at, b, q].reshape(16, CH_HI)
                    csend[p, 2 * b + g // 2, lax.rem(g, 2), q] = total.astype(BF)
            return carry

        lax.fori_loop(0, GROUPS, finish, 0)
        pltpu.make_async_copy(csend.at[p, i], out.at[p, i], recv_c.at[p]).start()

        def send_beams(step, inner):
            target = lax.rem(i + step, N)
            pltpu.make_async_remote_copy(
                src_ref=csend.at[p, target],
                dst_ref=out.at[p, i],
                send_sem=send_c.at[p],
                recv_sem=recv_c.at[p],
                device_id=(target, j),
                device_id_type=MESH,
            ).start()
            return inner

        lax.fori_loop(1, N, send_beams, 0)

    for p in range(2):
        beams(p)

    wait_voltages_sent(1)

    @pl.when(half == 0)
    def _():
        for p in range(2):
            relay(p).wait_send()

    def wait_sent(at, carry):
        fb = 4 * half + lax.rem(z + turn_of(lax.rem(at, 4)), 4)
        mine = fb == z

        @pl.when(mine)
        def _():
            part = chan.at[at, pl.ds(0, 2 * N - 1)]
            pltpu.make_async_copy(part, part, send_b.at[at]).wait()

        @pl.when(jnp.logical_not(mine))
        def _():
            pltpu.make_async_copy(chan.at[at], chan.at[at], send_b.at[at]).wait()

        return carry

    lax.fori_loop(0, STEPS, wait_sent, 0)
    for p in range(2):
        part = csend.at[p, pl.ds(0, N - 1)]
        pltpu.make_async_copy(part, part, send_c.at[p]).wait()
        pltpu.make_async_copy(csend.at[p], csend.at[p], recv_c.at[p]).wait()


def body(voltages, delay_table, beam_pointing, station_group):
    stations_here = voltages.shape[1]
    xv = voltages.reshape(2, stations_here, 2, FRAMES_OWN, CH_LO, CH_HI)

    vmem = pl.BlockSpec(memory_space=pltpu.VMEM)
    anywhere = pl.BlockSpec(memory_space=pl.ANY)
    out = pl.pallas_call(
        fused,
        out_shape=jax.ShapeDtypeStruct((2, N, 2, 2, 16, CH_HI), BF),
        in_specs=[pl.BlockSpec(memory_space=pltpu.SMEM), anywhere] + [vmem] * 6,
        out_specs=anywhere,
        scratch_shapes=[
            pltpu.VMEM((2, 2, 80, CH_LO, CH_HI), BF),
            pltpu.VMEM((512, 256), BF),
            pltpu.VMEM((CH_LO, 2, 8, 256), F32),
            pltpu.VMEM((512, 256), BF),
            pltpu.VMEM((STEPS, 2 * N, 16, 256), BF),
            pltpu.VMEM((128, 16, 256), BF),
            pltpu.VMEM((128, 16, 256), BF),
            pltpu.VMEM((8, 128), F32),
            pltpu.VMEM((128, 2, 2, BB, CH_HI), F32),
            pltpu.VMEM((8, CH_HI), jnp.int32),
            pltpu.VMEM((128, BB, 2, 2, 8, CH_HI), F32),
            pltpu.VMEM((2, N, 2, 2, 16, CH_HI), BF),
            pltpu.SMEM((8, CH_HI), jnp.int32),
            pltpu.SemaphoreType.DMA,
            pltpu.SemaphoreType.REGULAR,
            pltpu.SemaphoreType.DMA((2,)),
            pltpu.SemaphoreType.DMA((2,)),
            pltpu.SemaphoreType.DMA((2,)),
            pltpu.SemaphoreType.DMA((2,)),
            pltpu.SemaphoreType.DMA((STEPS,)),
            pltpu.SemaphoreType.DMA((2, N)),
            pltpu.SemaphoreType.DMA((2,)),
            pltpu.SemaphoreType.DMA((2,)),
        ],
        compiler_params=pltpu.CompilerParams(
            has_side_effects=True, collective_id=0, vmem_limit_bytes=40 * 1024 * 1024
        ),
        name="channelize_and_beamform",
    )(
        beam_pointing, xv, filter_window(), low_matrix(), high_matrix(), twiddle_table(),
        delay_table, station_group.reshape(1, -1),
    )

    out = out.reshape(2, N, 2, 2, 2, 8, CH_HI).transpose(2, 3, 0, 1, 5, 4, 6)
    return out.reshape(2, 2, 2, 128, 2, CH_HI)


def solution(mesh):
    in_specs = (P(None, "stn", None, "tf"), P(), P(), P())
    out_specs = P("stn", None, None, None, "tf", None)
    return jax.shard_map(body, mesh=mesh, in_specs=in_specs, out_specs=out_specs, check_vma=False)
```

```python
import math

import jax
import jax.numpy as jnp
import numpy as np
from jax import lax
from jax.experimental import pallas as pl
from jax.experimental.pallas import tpu as pltpu
from jax.sharding import PartitionSpec as P

TAPS = 16
CH_LO = 32
CH_HI = 128
POINTS = CH_LO * CH_HI
GROUPS = 4
TWO_PI = 2.0 * math.pi
BF = jnp.bfloat16
F32 = jnp.float32
MESH = pl.DeviceIdType.MESH

N = 16
FRAMES_OWN = 8
STEPS = 8
BB = 8


def filter_window():
    position = np.arange(TAPS * POINTS, dtype=np.float64)
    total = float(TAPS * POINTS)
    taper = 0.5 - 0.5 * np.cos(2.0 * np.pi / total * position)
    kernel = np.sinc((position - 0.5 * total) / POINTS) * taper
    return jnp.asarray(kernel.reshape(TAPS, CH_LO, CH_HI).astype(np.float32))


def dft_table(points):
    counter = np.arange(points)
    angles = 2.0 * np.pi / points * (counter[:, None] * counter[None, :] % points)
    cosine = np.cos(angles) / math.sqrt(points)
    sine = np.sin(angles) / math.sqrt(points)
    return np.stack([np.stack([cosine, sine]), np.stack([-sine, cosine])])


def low_matrix():
    table = dft_table(CH_LO)
    eye = np.eye(8)
    full = np.einsum("oqkn,fg->kofgqn", table, eye)
    return jnp.asarray(full.reshape(512, 512).astype(np.float32)).astype(BF)


def high_matrix():
    table = dft_table(CH_HI)
    return jnp.asarray(
        table.transpose(1, 2, 0, 3).reshape(256, 256).astype(np.float32)
    ).astype(BF)


def twiddle_table():
    angle = 2.0 * np.pi / POINTS * (np.arange(CH_LO)[:, None] * np.arange(CH_HI)[None, :])
    pair = np.stack([np.cos(angle), np.sin(angle)], axis=1)
    return jnp.asarray(np.concatenate([pair, pair], axis=-1).astype(np.float32))


def turn_parts(turns):
    t = (turns - jnp.round(turns)) * math.pi
    y = t * t
    s = t * (
        1.0
        + y
        * (
            -1.0 / 6
            + y
            * (
                1.0 / 120
                + y * (-1.0 / 5040 + y * (1.0 / 362880 + y * (-1.0 / 39916800 + y / 6227020800.0)))
            )
        )
    )
    c = 1.0 + y * (
        -0.5
        + y
        * (
            1.0 / 24
            + y
            * (
                -1.0 / 720
                + y * (1.0 / 40320 + y * (-1.0 / 3628800 + y * (1.0 / 479001600)))
            )
        )
    )
    return 1.0 - 2.0 * s * s, 2.0 * s * c


def turn_of(step):
    return lax.rem(step, 4)


def fused(
    pointing, xv, win, low, high, twid, table, group,
    out,
    rbuf, filt, first, rotated, chan, recv_0, recv_1, delay, weights, order, running, csend,
    order_smem, order_sem, entered, send_a, recv_a, send_r, recv_r, send_b, recv_b, send_c, recv_c,
):
    i = lax.axis_index("stn")
    j = lax.axis_index("tf")
    z = i // 2
    recv = (recv_0, recv_1)
    station, half = j // 2, lax.rem(j, 2)
    own_half = j // 8
    keeps = own_half == half

    barrier = pltpu.get_barrier_semaphore()

    def greet(step, carry):
        pl.semaphore_signal(
            barrier, inc=1, device_id=(i, lax.rem(j + step, N)), device_id_type=MESH
        )
        pl.semaphore_signal(
            barrier, inc=1, device_id=(lax.rem(i + step, N), j), device_id_type=MESH
        )
        return carry

    lax.fori_loop(1, N, greet, 0)
    pl.semaphore_wait(barrier, 2 * (N - 1))

    def send_voltages(p):
        block = pl.ds(16 + 8 * lax.rem(j, 8), 8)

        def send(step, carry):
            s_to = lax.rem(station + step, 8)
            j_to = 2 * s_to + own_half

            @pl.when(j_to == j)
            def _():
                pltpu.make_async_copy(xv.at[:, s_to, p], rbuf.at[p, :, block], recv_a.at[p]).start()

            @pl.when(j_to != j)
            def _():
                pltpu.make_async_remote_copy(
                    src_ref=xv.at[:, s_to, p],
                    dst_ref=rbuf.at[p, :, block],
                    send_sem=send_a.at[p],
                    recv_sem=recv_a.at[p],
                    device_id=(i, j_to),
                    device_id_type=MESH,
                ).start()

            return carry

        lax.fori_loop(0, 8, send, 0)

    def wait_voltages_sent(p):
        @pl.when(keeps)
        def _():
            part = rbuf.at[p, :, pl.ds(0, 56)]
            pltpu.make_async_copy(part, part, send_a.at[p]).wait()

        @pl.when(jnp.logical_not(keeps))
        def _():
            part = rbuf.at[p, :, pl.ds(0, 64)]
            pltpu.make_async_copy(part, part, send_a.at[p]).wait()

    def relay(p):
        return pltpu.make_async_remote_copy(
            src_ref=rbuf.at[p, :, pl.ds(64, 16)],
            dst_ref=rbuf.at[p, :, pl.ds(0, 16)],
            send_sem=send_r.at[p],
            recv_sem=recv_r.at[p],
            device_id=(i, j + 1),
            device_id_type=MESH,
        )

    def take_voltages(p):
        part = rbuf.at[p, :, pl.ds(16, 64)]
        pltpu.make_async_copy(part, part, recv_a.at[p]).wait()

        @pl.when(half == 0)
        def _():
            relay(p).start()

    send_voltages(0)

    def tell(step, carry):
        pl.semaphore_signal(
            entered, inc=1, device_id=(i, lax.rem(j + step, N)), device_id_type=MESH
        )
        return carry

    lax.fori_loop(1, N, tell, 0)

    @pl.when(half == 0)
    def _():
        rbuf[:, :, pl.ds(0, 16)] = jnp.zeros((2, 2, 16, CH_LO, CH_HI), BF)

    groups = group[...]
    for b in range(BB):
        row = jnp.zeros((1, CH_HI), F32)
        for g in range(GROUPS):
            row = jnp.where(groups == g, table[pl.ds(pointing[4 * b + g], 1), :], row)
        delay[pl.ds(b, 1), :] = row
    lane = lax.broadcasted_iota(jnp.int32, (8, CH_HI), 1)

    wide = jnp.broadcast_to(groups, (128, CH_HI))
    lanes = lax.broadcasted_iota(jnp.int32, (128, CH_HI), 1)
    rows = lax.broadcasted_iota(jnp.int32, (128, CH_HI), 0)
    own = jnp.sum(jnp.where(rows == lanes, wide, 0), axis=1, keepdims=True)
    ahead = jnp.logical_or(wide < own, jnp.logical_and(wide == own, lanes < rows))
    place = jnp.sum(jnp.where(ahead, 1, 0), axis=1, keepdims=True)
    starts = jnp.sum(jnp.where(own < lanes, 1, 0), axis=0, keepdims=True)
    opens = jnp.zeros((1, CH_HI), jnp.int32)
    for g in range(GROUPS):
        opens = jnp.where(starts[:, g : g + 1] == lanes[:1], 1, opens)
    order[...] = jnp.zeros((8, CH_HI), jnp.int32)
    order[pl.ds(0, 1), :] = jnp.sum(jnp.where(place == lanes, rows, 0), axis=0, keepdims=True)
    order[pl.ds(1, 1), :] = opens
    order[pl.ds(2, 1), :] = starts
    order[pl.ds(3, 1), :] = jnp.sum(jnp.where(own <= lanes, 1, 0), axis=0, keepdims=True)
    order_copy = pltpu.make_async_copy(order, order_smem, order_sem)
    order_copy.start()

    def make_weights(part, carry):
        for more in range(4):
            s = part * 4 + more
            here = lane == s
            column = jnp.sum(jnp.where(here, delay[...], 0.0), axis=1, keepdims=True)
            for k2 in range(2):
                channel = (2 * j + k2) + CH_LO * lane
                fraction = channel.astype(F32) * (1.0 / POINTS)
                cosine, sine = turn_parts(column * fraction)
                scale = math.sqrt(GROUPS / 128)
                weights[s, k2, 0] = (scale * cosine).astype(BF).astype(F32)
                weights[s, k2, 1] = (-scale * sine).astype(BF).astype(F32)
        return carry

    lax.fori_loop(0, 32, make_weights, 0)
    order_copy.wait()
    wait_voltages_sent(0)
    send_voltages(1)
    pl.semaphore_wait(entered, N - 1)

    def block(p, step):
        at = 4 * p + step
        near = lax.rem(z + turn_of(step), 4)

        @pl.when(jnp.logical_and(half == 1, near == 0))
        def _():
            part = rbuf.at[p, :, pl.ds(0, 16)]
            pltpu.make_async_copy(part, part, recv_r.at[p]).wait()

        fb = 4 * half + near

        def filter_part(part, inner):
            q = part // 2
            row = pl.multiple_of((part % 2) * 16, 16)
            for g2 in range(2):
                base = near * 16 + g2 * 8
                sums = [None] * 8
                taps = [win[t, pl.ds(row, 16), :] for t in range(TAPS)]
                for k in range(1, 24):
                    x = rbuf[p, q, base + k, pl.ds(row, 16), :].astype(F32)
                    for f in range(8):
                        t = k - 1 - f
                        if 0 <= t < TAPS:
                            term = taps[t] * x
                            sums[f] = term if sums[f] is None else sums[f] + term
                for f in range(8):
                    to = pl.ds(pl.multiple_of(f * 64 + q * 32 + row, 16), 16)
                    filt[to, pl.ds(128 * g2, 128)] = sums[f].astype(BF)
            return inner

        lax.fori_loop(0, 4, filter_part, 0)

        first[...] = jnp.dot(low[...], filt[...], preferred_element_type=F32).reshape(32, 2, 8, 256)

        def turn(c, inner):
            part = pl.ds(c * 8, 8)
            real, imag = first[part, 0], first[part, 1]
            cosine, sine = twid[part, 0:1, :], twid[part, 1:2, :]
            re = real * cosine + imag * sine
            im = imag * cosine - real * sine
            for g2 in range(2):
                lanes = slice(128 * g2, 128 * g2 + 128)
                both = jnp.concatenate([re[:, :, lanes], im[:, :, lanes]], axis=2).reshape(64, 256)
                rotated[pl.ds(pl.multiple_of(256 * g2 + 64 * c, 64), 64), :] = both.astype(BF)
            return inner

        lax.fori_loop(0, 4, turn, 0)
        done = jnp.dot(rotated[...], high[...], preferred_element_type=F32)
        chan[at] = done.astype(BF).reshape(2 * N, 16, 256)

        def send(n, inner):
            j_to = lax.rem(j + n, N)
            for g2 in range(2):
                here = jnp.logical_and(2 * fb + g2 == i, j_to == j)
                source = chan.at[at, N * g2 + j_to]
                target = recv[p].at[8 * i + station]

                @pl.when(here)
                def _():
                    pltpu.make_async_copy(source, target, recv_b.at[p, i]).start()

                @pl.when(jnp.logical_not(here))
                def _():
                    pltpu.make_async_remote_copy(
                        src_ref=source,
                        dst_ref=target,
                        send_sem=send_b.at[at],
                        recv_sem=recv_b.at[p, i],
                        device_id=(2 * fb + g2, j_to),
                        device_id_type=MESH,
                    ).start()

            return inner

        lax.fori_loop(0, N, send, 0)

    for p in range(2):
        take_voltages(p)

        def blocks(step, carry, p=p):
            block(p, step)
            return carry

        lax.fori_loop(0, 4, blocks, 0)

    def beams(p):
        def arrive(i_from, carry):
            part = recv[p].at[pl.ds(8 * i_from, 8)]
            pltpu.make_async_copy(part, part, recv_b.at[p, i_from]).wait()
            return carry

        lax.fori_loop(0, N, arrive, 0)

        def add(m, sums):
            s = order_smem[0, m]
            keep = jnp.where(order_smem[1, m] > 0, 0.0, 1.0)
            value = recv[p][s].astype(F32)
            result = []
            for k2 in range(2):
                vr = value[8 * k2 : 8 * k2 + 8, :128]
                vi = value[8 * k2 : 8 * k2 + 8, 128:]
                for b in range(BB):
                    wr = weights[s, k2, 0, pl.ds(b, 1), :]
                    wi = weights[s, k2, 1, pl.ds(b, 1), :]
                    re, im = sums[2 * (BB * k2 + b)], sums[2 * (BB * k2 + b) + 1]
                    re = keep * re + (wr * vr - wi * vi)
                    im = keep * im + (wr * vi + wi * vr)
                    running[m, b, 0, k2] = re
                    running[m, b, 1, k2] = im
                    result += [re, im]
            return tuple(result)

        zero = jnp.zeros((8, CH_HI), F32)

        def add_some(part, sums):
            for more in range(2):
                sums = add(part * 2 + more, sums)
            return sums

        lax.fori_loop(0, 128 // 2, add_some, (zero,) * (4 * BB))

        def finish(g, carry):
            start, stop = order_smem[2, g], order_smem[3, g]
            some = jnp.where(stop > start, 1.0, 0.0)
            at = jnp.maximum(stop - 1, 0)
            for b in range(BB):
                for q in range(2):
                    total = some * running[at, b, q].reshape(16, CH_HI)
                    csend[p, 2 * b + g // 2, lax.rem(g, 2), q] = total.astype(BF)
            return carry

        lax.fori_loop(0, GROUPS, finish, 0)
        pltpu.make_async_copy(csend.at[p, i], out.at[p, i], recv_c.at[p]).start()

        def send_beams(step, inner):
            target = lax.rem(i + step, N)
            pltpu.make_async_remote_copy(
                src_ref=csend.at[p, target],
                dst_ref=out.at[p, i],
                send_sem=send_c.at[p],
                recv_sem=recv_c.at[p],
                device_id=(target, j),
                device_id_type=MESH,
            ).start()
            return inner

        lax.fori_loop(1, N, send_beams, 0)

    for p in range(2):
        beams(p)

    wait_voltages_sent(1)

    @pl.when(half == 0)
    def _():
        for p in range(2):
            relay(p).wait_send()

    def wait_sent(at, carry):
        fb = 4 * half + lax.rem(z + turn_of(lax.rem(at, 4)), 4)
        mine = fb == z

        @pl.when(mine)
        def _():
            part = chan.at[at, pl.ds(0, 2 * N - 1)]
            pltpu.make_async_copy(part, part, send_b.at[at]).wait()

        @pl.when(jnp.logical_not(mine))
        def _():
            pltpu.make_async_copy(chan.at[at], chan.at[at], send_b.at[at]).wait()

        return carry

    lax.fori_loop(0, STEPS, wait_sent, 0)
    for p in range(2):
        part = csend.at[p, pl.ds(0, N - 1)]
        pltpu.make_async_copy(part, part, send_c.at[p]).wait()
        pltpu.make_async_copy(csend.at[p], csend.at[p], recv_c.at[p]).wait()


def body(voltages, delay_table, beam_pointing, station_group):
    stations_here = voltages.shape[1]
    xv = voltages.reshape(2, stations_here, 2, FRAMES_OWN, CH_LO, CH_HI)

    vmem = pl.BlockSpec(memory_space=pltpu.VMEM)
    anywhere = pl.BlockSpec(memory_space=pl.ANY)
    out = pl.pallas_call(
        fused,
        out_shape=jax.ShapeDtypeStruct((2, N, 2, 2, 16, CH_HI), BF),
        in_specs=[pl.BlockSpec(memory_space=pltpu.SMEM), anywhere] + [vmem] * 6,
        out_specs=anywhere,
        scratch_shapes=[
            pltpu.VMEM((2, 2, 80, CH_LO, CH_HI), BF),
            pltpu.VMEM((512, 256), BF),
            pltpu.VMEM((CH_LO, 2, 8, 256), F32),
            pltpu.VMEM((512, 256), BF),
            pltpu.VMEM((STEPS, 2 * N, 16, 256), BF),
            pltpu.VMEM((128, 16, 256), BF),
            pltpu.VMEM((128, 16, 256), BF),
            pltpu.VMEM((8, 128), F32),
            pltpu.VMEM((128, 2, 2, BB, CH_HI), F32),
            pltpu.VMEM((8, CH_HI), jnp.int32),
            pltpu.VMEM((128, BB, 2, 2, 8, CH_HI), F32),
            pltpu.VMEM((2, N, 2, 2, 16, CH_HI), BF),
            pltpu.SMEM((8, CH_HI), jnp.int32),
            pltpu.SemaphoreType.DMA,
            pltpu.SemaphoreType.REGULAR,
            pltpu.SemaphoreType.DMA((2,)),
            pltpu.SemaphoreType.DMA((2,)),
            pltpu.SemaphoreType.DMA((2,)),
            pltpu.SemaphoreType.DMA((2,)),
            pltpu.SemaphoreType.DMA((STEPS,)),
            pltpu.SemaphoreType.DMA((2, N)),
            pltpu.SemaphoreType.DMA((2,)),
            pltpu.SemaphoreType.DMA((2,)),
        ],
        compiler_params=pltpu.CompilerParams(
            has_side_effects=True, collective_id=0, vmem_limit_bytes=40 * 1024 * 1024
        ),
        name="channelize_and_beamform",
    )(
        beam_pointing, xv, filter_window(), low_matrix(), high_matrix(), twiddle_table(),
        delay_table, station_group.reshape(1, -1),
    )

    out = out.reshape(2, N, 2, 2, 2, 8, CH_HI).transpose(2, 3, 0, 1, 5, 4, 6)
    return out.reshape(2, 2, 2, 128, 2, CH_HI)


def solution(mesh):
    in_specs = (P(None, "stn", None, "tf"), P(), P(), P())
    out_specs = P("stn", None, None, None, "tf", None)
    return jax.shard_map(body, mesh=mesh, in_specs=in_specs, out_specs=out_specs, check_vma=False)
```

```python
import math

import jax
import jax.numpy as jnp
import numpy as np
from jax import lax
from jax.experimental import pallas as pl
from jax.experimental.pallas import tpu as pltpu
from jax.sharding import PartitionSpec as P

TAPS = 16
CH_LO = 32
CH_HI = 128
POINTS = CH_LO * CH_HI
GROUPS = 4
TWO_PI = 2.0 * math.pi
BF = jnp.bfloat16
F32 = jnp.float32
MESH = pl.DeviceIdType.MESH

N = 16
FRAMES_OWN = 8
STEPS = 8
BB = 8


def filter_window():
    position = np.arange(TAPS * POINTS, dtype=np.float64)
    total = float(TAPS * POINTS)
    taper = 0.5 - 0.5 * np.cos(2.0 * np.pi / total * position)
    kernel = np.sinc((position - 0.5 * total) / POINTS) * taper
    return jnp.asarray(kernel.reshape(TAPS, CH_LO, CH_HI).astype(np.float32))


def dft_table(points):
    counter = np.arange(points)
    angles = 2.0 * np.pi / points * (counter[:, None] * counter[None, :] % points)
    cosine = np.cos(angles) / math.sqrt(points)
    sine = np.sin(angles) / math.sqrt(points)
    return np.stack([np.stack([cosine, sine]), np.stack([-sine, cosine])])


def low_matrix():
    table = dft_table(CH_LO)
    eye = np.eye(8)
    full = np.einsum("oqkn,fg->kofgqn", table, eye)
    return jnp.asarray(full.reshape(512, 512).astype(np.float32)).astype(BF)


def high_matrix():
    table = dft_table(CH_HI)
    return jnp.asarray(
        table.transpose(1, 2, 0, 3).reshape(256, 256).astype(np.float32)
    ).astype(BF)


def twiddle_table():
    angle = 2.0 * np.pi / POINTS * (np.arange(CH_LO)[:, None] * np.arange(CH_HI)[None, :])
    pair = np.stack([np.cos(angle), np.sin(angle)], axis=1)
    return jnp.asarray(np.concatenate([pair, pair], axis=-1).astype(np.float32))


def turn_parts(turns):
    t = (turns - jnp.round(turns)) * math.pi
    y = t * t
    s = t * (
        1.0
        + y
        * (
            -1.0 / 6
            + y
            * (
                1.0 / 120
                + y * (-1.0 / 5040 + y * (1.0 / 362880 + y * (-1.0 / 39916800 + y / 6227020800.0)))
            )
        )
    )
    c = 1.0 + y * (
        -0.5
        + y
        * (
            1.0 / 24
            + y
            * (
                -1.0 / 720
                + y * (1.0 / 40320 + y * (-1.0 / 3628800 + y * (1.0 / 479001600)))
            )
        )
    )
    return 1.0 - 2.0 * s * s, 2.0 * s * c


def turn_of(step):
    return lax.rem(step, 4)


def fused(
    pointing, xv, win, low, high, twid, table, group,
    out,
    rbuf, filt, first, rotated, chan, recv_0, recv_1, delay, weights, order, running, csend,
    order_smem, order_sem, entered, send_a, recv_a, send_r, recv_r, send_b, recv_b, send_c, recv_c,
):
    i = lax.axis_index("stn")
    j = lax.axis_index("tf")
    z = i // 2
    recv = (recv_0, recv_1)
    station, half = j // 2, lax.rem(j, 2)
    own_half = j // 8
    keeps = own_half == half

    barrier = pltpu.get_barrier_semaphore()

    def greet(step, carry):
        pl.semaphore_signal(
            barrier, inc=1, device_id=(i, lax.rem(j + step, N)), device_id_type=MESH
        )
        pl.semaphore_signal(
            barrier, inc=1, device_id=(lax.rem(i + step, N), j), device_id_type=MESH
        )
        return carry

    lax.fori_loop(1, N, greet, 0)
    pl.semaphore_wait(barrier, 2 * (N - 1))

    def send_voltages(p):
        block = pl.ds(16 + 8 * lax.rem(j, 8), 8)

        def send(step, carry):
            s_to = lax.rem(station + step, 8)
            j_to = 2 * s_to + own_half

            @pl.when(j_to == j)
            def _():
                pltpu.make_async_copy(xv.at[:, s_to, p], rbuf.at[p, :, block], recv_a.at[p]).start()

            @pl.when(j_to != j)
            def _():
                pltpu.make_async_remote_copy(
                    src_ref=xv.at[:, s_to, p],
                    dst_ref=rbuf.at[p, :, block],
                    send_sem=send_a.at[p],
                    recv_sem=recv_a.at[p],
                    device_id=(i, j_to),
                    device_id_type=MESH,
                ).start()

            return carry

        lax.fori_loop(0, 8, send, 0)

    def wait_voltages_sent(p):
        @pl.when(keeps)
        def _():
            part = rbuf.at[p, :, pl.ds(0, 56)]
            pltpu.make_async_copy(part, part, send_a.at[p]).wait()

        @pl.when(jnp.logical_not(keeps))
        def _():
            part = rbuf.at[p, :, pl.ds(0, 64)]
            pltpu.make_async_copy(part, part, send_a.at[p]).wait()

    def relay(p):
        return pltpu.make_async_remote_copy(
            src_ref=rbuf.at[p, :, pl.ds(64, 16)],
            dst_ref=rbuf.at[p, :, pl.ds(0, 16)],
            send_sem=send_r.at[p],
            recv_sem=recv_r.at[p],
            device_id=(i, j + 1),
            device_id_type=MESH,
        )

    def take_voltages(p):
        part = rbuf.at[p, :, pl.ds(16, 64)]
        pltpu.make_async_copy(part, part, recv_a.at[p]).wait()

        @pl.when(half == 0)
        def _():
            relay(p).start()

    send_voltages(0)

    def tell(step, carry):
        pl.semaphore_signal(
            entered, inc=1, device_id=(i, lax.rem(j + step, N)), device_id_type=MESH
        )
        return carry

    lax.fori_loop(1, N, tell, 0)

    @pl.when(half == 0)
    def _():
        rbuf[:, :, pl.ds(0, 16)] = jnp.zeros((2, 2, 16, CH_LO, CH_HI), BF)

    groups = group[...]
    for b in range(BB):
        row = jnp.zeros((1, CH_HI), F32)
        for g in range(GROUPS):
            row = jnp.where(groups == g, table[pl.ds(pointing[4 * b + g], 1), :], row)
        delay[pl.ds(b, 1), :] = row
    lane = lax.broadcasted_iota(jnp.int32, (8, CH_HI), 1)

    wide = jnp.broadcast_to(groups, (128, CH_HI))
    lanes = lax.broadcasted_iota(jnp.int32, (128, CH_HI), 1)
    rows = lax.broadcasted_iota(jnp.int32, (128, CH_HI), 0)
    own = jnp.sum(jnp.where(rows == lanes, wide, 0), axis=1, keepdims=True)
    ahead = jnp.logical_or(wide < own, jnp.logical_and(wide == own, lanes < rows))
    place = jnp.sum(jnp.where(ahead, 1, 0), axis=1, keepdims=True)
    starts = jnp.sum(jnp.where(own < lanes, 1, 0), axis=0, keepdims=True)
    opens = jnp.zeros((1, CH_HI), jnp.int32)
    for g in range(GROUPS):
        opens = jnp.where(starts[:, g : g + 1] == lanes[:1], 1, opens)
    order[...] = jnp.zeros((8, CH_HI), jnp.int32)
    order[pl.ds(0, 1), :] = jnp.sum(jnp.where(place == lanes, rows, 0), axis=0, keepdims=True)
    order[pl.ds(1, 1), :] = opens
    order[pl.ds(2, 1), :] = starts
    order[pl.ds(3, 1), :] = jnp.sum(jnp.where(own <= lanes, 1, 0), axis=0, keepdims=True)
    order_copy = pltpu.make_async_copy(order, order_smem, order_sem)
    order_copy.start()

    def make_weights(part, carry):
        for more in range(4):
            s = part * 4 + more
            here = lane == s
            column = jnp.sum(jnp.where(here, delay[...], 0.0), axis=1, keepdims=True)
            for k2 in range(2):
                channel = (2 * j + k2) + CH_LO * lane
                fraction = channel.astype(F32) * (1.0 / POINTS)
                cosine, sine = turn_parts(column * fraction)
                scale = math.sqrt(GROUPS / 128)
                weights[s, k2, 0] = (scale * cosine).astype(BF).astype(F32)
                weights[s, k2, 1] = (-scale * sine).astype(BF).astype(F32)
        return carry

    lax.fori_loop(0, 32, make_weights, 0)
    order_copy.wait()
    wait_voltages_sent(0)
    send_voltages(1)
    pl.semaphore_wait(entered, N - 1)

    def block(p, step):
        at = 4 * p + step
        near = lax.rem(z + turn_of(step), 4)

        @pl.when(jnp.logical_and(half == 1, near == 0))
        def _():
            part = rbuf.at[p, :, pl.ds(0, 16)]
            pltpu.make_async_copy(part, part, recv_r.at[p]).wait()

        fb = 4 * half + near

        def filter_part(part, inner):
            q = part // 2
            row = pl.multiple_of((part % 2) * 16, 16)
            for g2 in range(2):
                base = near * 16 + g2 * 8
                sums = [None] * 8
                taps = [win[t, pl.ds(row, 16), :] for t in range(TAPS)]
                for k in range(1, 24):
                    x = rbuf[p, q, base + k, pl.ds(row, 16), :].astype(F32)
                    for f in range(8):
                        t = k - 1 - f
                        if 0 <= t < TAPS:
                            term = taps[t] * x
                            sums[f] = term if sums[f] is None else sums[f] + term
                for f in range(8):
                    to = pl.ds(pl.multiple_of(f * 64 + q * 32 + row, 16), 16)
                    filt[to, pl.ds(128 * g2, 128)] = sums[f].astype(BF)
            return inner

        lax.fori_loop(0, 4, filter_part, 0)

        first[...] = jnp.dot(low[...], filt[...], preferred_element_type=F32).reshape(32, 2, 8, 256)

        def turn(c, inner):
            part = pl.ds(c * 8, 8)
            real, imag = first[part, 0], first[part, 1]
            cosine, sine = twid[part, 0:1, :], twid[part, 1:2, :]
            re = real * cosine + imag * sine
            im = imag * cosine - real * sine
            for g2 in range(2):
                lanes = slice(128 * g2, 128 * g2 + 128)
                both = jnp.concatenate([re[:, :, lanes], im[:, :, lanes]], axis=2).reshape(64, 256)
                rotated[pl.ds(pl.multiple_of(256 * g2 + 64 * c, 64), 64), :] = both.astype(BF)
            return inner

        lax.fori_loop(0, 4, turn, 0)
        done = jnp.dot(rotated[...], high[...], preferred_element_type=F32)
        chan[at] = done.astype(BF).reshape(2 * N, 16, 256)

        def send(n, inner):
            j_to = lax.rem(j + n, N)
            for g2 in range(2):
                here = jnp.logical_and(2 * fb + g2 == i, j_to == j)
                source = chan.at[at, N * g2 + j_to]
                target = recv[p].at[8 * i + station]

                @pl.when(here)
                def _():
                    pltpu.make_async_copy(source, target, recv_b.at[p, i]).start()

                @pl.when(jnp.logical_not(here))
                def _():
                    pltpu.make_async_remote_copy(
                        src_ref=source,
                        dst_ref=target,
                        send_sem=send_b.at[at],
                        recv_sem=recv_b.at[p, i],
                        device_id=(2 * fb + g2, j_to),
                        device_id_type=MESH,
                    ).start()

            return inner

        lax.fori_loop(0, N, send, 0)

    for p in range(2):
        take_voltages(p)

        def blocks(step, carry, p=p):
            block(p, step)
            return carry

        lax.fori_loop(0, 4, blocks, 0)

    def beams(p):
        def arrive(i_from, carry):
            part = recv[p].at[pl.ds(8 * i_from, 8)]
            pltpu.make_async_copy(part, part, recv_b.at[p, i_from]).wait()
            return carry

        lax.fori_loop(0, N, arrive, 0)

        def add(m, sums):
            s = order_smem[0, m]
            keep = jnp.where(order_smem[1, m] > 0, 0.0, 1.0)
            value = recv[p][s].astype(F32)
            result = []
            for k2 in range(2):
                vr = value[8 * k2 : 8 * k2 + 8, :128]
                vi = value[8 * k2 : 8 * k2 + 8, 128:]
                for b in range(BB):
                    wr = weights[s, k2, 0, pl.ds(b, 1), :]
                    wi = weights[s, k2, 1, pl.ds(b, 1), :]
                    re, im = sums[2 * (BB * k2 + b)], sums[2 * (BB * k2 + b) + 1]
                    re = keep * re + (wr * vr - wi * vi)
                    im = keep * im + (wr * vi + wi * vr)
                    running[m, b, 0, k2] = re
                    running[m, b, 1, k2] = im
                    result += [re, im]
            return tuple(result)

        zero = jnp.zeros((8, CH_HI), F32)

        def add_some(part, sums):
            for more in range(4):
                sums = add(part * 4 + more, sums)
            return sums

        lax.fori_loop(0, 128 // 4, add_some, (zero,) * (4 * BB))

        def finish(g, carry):
            start, stop = order_smem[2, g], order_smem[3, g]
            some = jnp.where(stop > start, 1.0, 0.0)
            at = jnp.maximum(stop - 1, 0)
            for b in range(BB):
                for q in range(2):
                    total = some * running[at, b, q].reshape(16, CH_HI)
                    csend[p, 2 * b + g // 2, lax.rem(g, 2), q] = total.astype(BF)
            return carry

        lax.fori_loop(0, GROUPS, finish, 0)
        pltpu.make_async_copy(csend.at[p, i], out.at[p, i], recv_c.at[p]).start()

        def send_beams(step, inner):
            target = lax.rem(i + step, N)
            pltpu.make_async_remote_copy(
                src_ref=csend.at[p, target],
                dst_ref=out.at[p, i],
                send_sem=send_c.at[p],
                recv_sem=recv_c.at[p],
                device_id=(target, j),
                device_id_type=MESH,
            ).start()
            return inner

        lax.fori_loop(1, N, send_beams, 0)

    for p in range(2):
        beams(p)

    wait_voltages_sent(1)

    @pl.when(half == 0)
    def _():
        for p in range(2):
            relay(p).wait_send()

    def wait_sent(at, carry):
        fb = 4 * half + lax.rem(z + turn_of(lax.rem(at, 4)), 4)
        mine = fb == z

        @pl.when(mine)
        def _():
            part = chan.at[at, pl.ds(0, 2 * N - 1)]
            pltpu.make_async_copy(part, part, send_b.at[at]).wait()

        @pl.when(jnp.logical_not(mine))
        def _():
            pltpu.make_async_copy(chan.at[at], chan.at[at], send_b.at[at]).wait()

        return carry

    lax.fori_loop(0, STEPS, wait_sent, 0)
    for p in range(2):
        part = csend.at[p, pl.ds(0, N - 1)]
        pltpu.make_async_copy(part, part, send_c.at[p]).wait()
        pltpu.make_async_copy(csend.at[p], csend.at[p], recv_c.at[p]).wait()


def body(voltages, delay_table, beam_pointing, station_group):
    stations_here = voltages.shape[1]
    xv = voltages.reshape(2, stations_here, 2, FRAMES_OWN, CH_LO, CH_HI)

    vmem = pl.BlockSpec(memory_space=pltpu.VMEM)
    anywhere = pl.BlockSpec(memory_space=pl.ANY)
    out = pl.pallas_call(
        fused,
        out_shape=jax.ShapeDtypeStruct((2, N, 2, 2, 16, CH_HI), BF),
        in_specs=[pl.BlockSpec(memory_space=pltpu.SMEM), anywhere] + [vmem] * 6,
        out_specs=anywhere,
        scratch_shapes=[
            pltpu.VMEM((2, 2, 80, CH_LO, CH_HI), BF),
            pltpu.VMEM((512, 256), BF),
            pltpu.VMEM((CH_LO, 2, 8, 256), F32),
            pltpu.VMEM((512, 256), BF),
            pltpu.VMEM((STEPS, 2 * N, 16, 256), BF),
            pltpu.VMEM((128, 16, 256), BF),
            pltpu.VMEM((128, 16, 256), BF),
            pltpu.VMEM((8, 128), F32),
            pltpu.VMEM((128, 2, 2, BB, CH_HI), F32),
            pltpu.VMEM((8, CH_HI), jnp.int32),
            pltpu.VMEM((128, BB, 2, 2, 8, CH_HI), F32),
            pltpu.VMEM((2, N, 2, 2, 16, CH_HI), BF),
            pltpu.SMEM((8, CH_HI), jnp.int32),
            pltpu.SemaphoreType.DMA,
            pltpu.SemaphoreType.REGULAR,
            pltpu.SemaphoreType.DMA((2,)),
            pltpu.SemaphoreType.DMA((2,)),
            pltpu.SemaphoreType.DMA((2,)),
            pltpu.SemaphoreType.DMA((2,)),
            pltpu.SemaphoreType.DMA((STEPS,)),
            pltpu.SemaphoreType.DMA((2, N)),
            pltpu.SemaphoreType.DMA((2,)),
            pltpu.SemaphoreType.DMA((2,)),
        ],
        compiler_params=pltpu.CompilerParams(
            has_side_effects=True, collective_id=0, vmem_limit_bytes=40 * 1024 * 1024
        ),
        name="channelize_and_beamform",
    )(
        beam_pointing, xv, filter_window(), low_matrix(), high_matrix(), twiddle_table(),
        delay_table, station_group.reshape(1, -1),
    )

    out = out.reshape(2, N, 2, 2, 2, 8, CH_HI).transpose(2, 3, 0, 1, 5, 4, 6)
    return out.reshape(2, 2, 2, 128, 2, CH_HI)


def solution(mesh):
    in_specs = (P(None, "stn", None, "tf"), P(), P(), P())
    out_specs = P("stn", None, None, None, "tf", None)
    return jax.shard_map(body, mesh=mesh, in_specs=in_specs, out_specs=out_specs, check_vma=False)
```
